32 devices in a mesh: dp: 4 (over x, core), seq: 8 (over z, y).
Axes of the slice: x: 2, y: 2, z: 4, core: 2. Of those that a mesh axis runs over, the one named last changes fastest.
Arguments:
- ssm_input: bfloat16 [4, 2048, 1024], P('dp', 'seq'), may hold values from -6 to 6
- gate_input: bfloat16 [4, 2048, 1024], P('dp', 'seq'), may hold values from -6 to 6
- state_proj: bfloat16 [4, 2048, 512], P('dp', 'seq'), may hold values from -6 to 6
- step_raw: float32 [4, 32, 2048], P('dp', None, 'seq'), may hold values from -5 to 400
- decay_log: float32 [2, 16], replicated, may hold values from -10 to 0
- skip_gain: float32 [16], replicated, may hold values from 0.5 to 2
- norm_gain: float32 [1024], replicated, may hold values from 0.25 to 1.75
- out_weight: bfloat16 [1024, 1024], P('dp'), may hold values from -0.1875 to 0.1875
- latents: bfloat16 [256, 1024], replicated, may hold values from -450 to 450
- lengths: int32 [4], P('dp'), may hold values from 1024 to 2048, as said below
Outputs:
- encoded: bfloat16 [4, 2048, 1024], P('dp', 'seq')
- pooled: bfloat16 [4, 256, 1024], P('dp')
The draws below stay inside these ranges and needn't reach their ends.
Inputs may be any that keep to these rules, and one draw needn't show every extreme that they name: `lengths`: positions at or after a sequence's length are padding; at least one sequence has none, and one has 1024 real tokens.
All inputs are finite; a program needn't handle non-finite values.
Results may differ from the reference program's by a relative error of at most 0.034.
Values may be sent and summed in bfloat16 or wider, within the bound.
A program may use at most 128 MiB of HBM per device.

```python
import math
import jax
import jax.numpy as jnp
from jax import lax

D = 1024
MIXER_HEADS = 16
P_SIZE = 64
STATE = 128
BLOCK = 128
R = 256
L_DEV = 256
HP = 1024
SEQUENCE_TOKENS = 2048
SEQUENCE_COUNT = 4


spike_total = 3


def common_lookup_tables(key):
    base_key = jax.random.fold_in(key, 4711)
    random_key_list = jax.random.split(base_key, 6)
    fast_chance = 0.5
    is_fast = jax.random.bernoulli(random_key_list[0], fast_chance, (2, MIXER_HEADS))
    slow_rate = 20.0 * jnp.exp(jax.random.uniform(random_key_list[1], (2, MIXER_HEADS), minval=math.log(0.3), maxval=0.0)) / SEQUENCE_TOKENS
    fast_rate = jnp.exp(jax.random.uniform(random_key_list[2], (2, MIXER_HEADS), minval=math.log(0.4), maxval=math.log(0.67)))
    forget_rate = jnp.where(is_fast, fast_rate, slow_rate)
    jolt_placement_slot = jax.random.randint(random_key_list[3], (SEQUENCE_COUNT, spike_total), 0, SEQUENCE_TOKENS)
    spike_loss = jax.random.uniform(random_key_list[4], (SEQUENCE_COUNT, 2 * MIXER_HEADS, spike_total), minval=0.2, maxval=0.45)
    return (forget_rate, jolt_placement_slot, spike_loss, random_key_list[5])


def draw_decay_log(key, part):
    forget_rate, unused_item, unused_item, unused_item = common_lookup_tables(key)
    return jnp.log(forget_rate)


def draw_step_raw(key, part):
    forget_rate, jolt_placement_slot, spike_loss, reserve_random_key = common_lookup_tables(key)
    first_key, second_key = jax.random.split(reserve_random_key)
    typical = jnp.exp(jax.random.uniform(first_key, (SEQUENCE_COUNT, 2 * MIXER_HEADS, SEQUENCE_TOKENS), minval=math.log(0.02), maxval=math.log(0.1)))
    factor = jnp.exp(jax.random.uniform(second_key, (SEQUENCE_COUNT, 2 * MIXER_HEADS, SEQUENCE_TOKENS // L_DEV), minval=math.log(0.5), maxval=math.log(2.0)))
    quantized_stride_width = typical * jnp.repeat(factor, L_DEV, axis=2)
    jolt_stride_amount = jnp.minimum(spike_loss / forget_rate.reshape(2 * MIXER_HEADS)[None, :, None], 400.0)
    symbol_offset = jnp.arange(SEQUENCE_TOKENS, dtype=jnp.int32)
    for jolt_ordinal in range(spike_total):
        within_outburst_range = symbol_offset[None, None, :] == jolt_placement_slot[:, jolt_ordinal][:, None, None]
        quantized_stride_width = jnp.where(within_outburst_range, jnp.maximum(quantized_stride_width, jolt_stride_amount[:, :, jolt_ordinal][:, :, None]), quantized_stride_width)
    return quantized_stride_width + jnp.log(-jnp.expm1(-quantized_stride_width))


def draw_state_proj(key, part):
    unused_item, jolt_placement_slot, unused_item, unused_item = common_lookup_tables(key)
    values = jnp.clip(jax.random.normal(jax.random.fold_in(key, 77), (SEQUENCE_COUNT, SEQUENCE_TOKENS, 4 * STATE)), -6.0, 6.0)
    symbol_offset = jnp.arange(SEQUENCE_TOKENS, dtype=jnp.int32)
    within_outburst_range = jnp.any(symbol_offset[None, None, :] == jolt_placement_slot[:, :, None], axis=1)
    column = jnp.arange(4 * STATE, dtype=jnp.int32)
    entering_mapping_vector = (column < STATE) | (column >= 2 * STATE) & (column < 3 * STATE)
    contraction_multiplier = jnp.where(within_outburst_range[:, :, None] & entering_mapping_vector[None, None, :], 0.01, 1.0)
    return (values * contraction_multiplier).astype(jnp.bfloat16)


def draw_latents(key, part):
    first_key = jax.random.fold_in(jax.random.fold_in(key, 31), 0)
    values = 2.5 * jnp.clip(jax.random.normal(first_key, (R, D)), -6.0, 6.0)
    return values.astype(jnp.bfloat16)


def draw_lengths(key, part):
    first_key, second_key = jax.random.split(jax.random.fold_in(key, 99))
    counts = jax.random.randint(first_key, (SEQUENCE_COUNT,), SEQUENCE_TOKENS // 2, SEQUENCE_TOKENS + 1)
    shuffled = jax.random.permutation(second_key, SEQUENCE_COUNT)
    counts = counts.at[shuffled[0]].set(SEQUENCE_TOKENS)
    counts = counts.at[shuffled[1]].set(SEQUENCE_TOKENS // 2)
    return counts.astype(jnp.int32)


def level_of(rng, dims, shards, low, top_value):
    loudness = 1.0
    for position, blocks in shards:
        draws = jax.random.uniform(jax.random.fold_in(jax.random.fold_in(rng, 6), position), (blocks,), jnp.float32, low / len(shards), top_value / len(shards))
        loudness = loudness * jnp.repeat(jnp.exp(draws), dims[position] // blocks).reshape((-1,) + (1,) * (len(dims) - 1 - position))
    return loudness


def normal_values(rng, dims, scale, limit, shards=(), held_as=jnp.bfloat16):
    values = jax.random.normal(rng, dims, jnp.float32) * scale
    if len(shards) > 0:
        values = level_of(rng, dims, shards, -0.22, 0.18) * values
    return jnp.clip(values, min=-limit, max=limit).astype(held_as)


def setup_inputs(seed: int = 0) -> dict:
    splits = jax.random.split(jax.random.key(seed), 11)
    ssm_input = normal_values(splits[0], (SEQUENCE_COUNT, SEQUENCE_TOKENS, HP), 1.0, 6.0, ((0, 4), (1, 8)))
    gate_input = normal_values(splits[1], (SEQUENCE_COUNT, SEQUENCE_TOKENS, HP), 1.0, 6.0, ((0, 4), (1, 8)))
    state_proj = draw_state_proj(jax.random.fold_in(splits[10], 71), 0)
    step_raw = draw_step_raw(jax.random.fold_in(splits[10], 71), 0)
    decay_log = draw_decay_log(jax.random.fold_in(splits[10], 71), 0)
    skip_gain = jnp.clip(jax.random.uniform(splits[5], (MIXER_HEADS,), jnp.float32, 0.5, 2.0), 0.5, 2.0)
    norm_gain = jnp.clip(1.0 + 0.15 * jax.random.normal(splits[6], (HP,), jnp.float32), 0.25, 1.75)
    out_weight = normal_values(splits[7], (HP, D), HP ** -0.5, 0.1875, ((0, 4),))
    latents = draw_latents(jax.random.fold_in(splits[10], 71), 0)
    lengths = draw_lengths(jax.random.fold_in(splits[10], 71), 0)
    return {"ssm_input": ssm_input, "gate_input": gate_input, "state_proj": state_proj, "step_raw": step_raw, "decay_log": decay_log, "skip_gain": skip_gain, "norm_gain": norm_gain, "out_weight": out_weight, "latents": latents, "lengths": lengths}


def block_terms(x_block, dt_block, b_block, c_block, forget_rate):
    cumulative = jnp.cumsum(-dt_block * forget_rate[:, None], axis=1)
    gram_matrix = jnp.dot(c_block, b_block.T, preferred_element_type=jnp.float32)
    symbol_offset = jnp.arange(x_block.shape[0], dtype=jnp.int32)
    causal = symbol_offset[:, None] >= symbol_offset[None, :]
    spread = jnp.where(causal[None], cumulative[:, :, None] - cumulative[:, None, :], -jnp.inf)
    mixing = (gram_matrix[None] * jnp.exp(spread) * dt_block[:, None, :]).astype(jnp.bfloat16)
    mixing = lax.optimization_barrier(mixing)
    intra_out = jnp.einsum('hqk,khp->qhp', mixing.astype(jnp.float32), x_block.astype(jnp.float32))
    tail_weight = jnp.exp(cumulative[:, -1:] - cumulative) * dt_block
    scaled_x = (x_block.astype(jnp.float32) * tail_weight.T[:, :, None]).astype(jnp.bfloat16)
    scaled_x = lax.optimization_barrier(scaled_x)
    contrib = jnp.einsum('khp,kn->hpn', scaled_x.astype(jnp.float32), b_block.astype(jnp.float32))
    return (intra_out, cumulative, contrib)

def scan_sequence(x_seq, dt_seq, b_seq, c_seq, forget_rate):
    block_count = x_seq.shape[0] // BLOCK
    x_blocks = x_seq.reshape(block_count, BLOCK, MIXER_HEADS, P_SIZE)
    dt_blocks = dt_seq.reshape(MIXER_HEADS, block_count, BLOCK).transpose(1, 0, 2)
    b_blocks = b_seq.reshape(block_count, BLOCK, STATE)
    c_blocks = c_seq.reshape(block_count, BLOCK, STATE)

    def block_step(carried, inputs):
        x_block, dt_block, b_block, c_block = inputs
        intra_out, cumulative, contrib = block_terms(x_block, dt_block, b_block, c_block, forget_rate)
        held_state = lax.optimization_barrier(carried.astype(jnp.bfloat16))
        state_out = jnp.einsum('qn,hpn->qhp', c_block.astype(jnp.float32), held_state.astype(jnp.float32))
        result = intra_out + state_out * jnp.exp(cumulative).T[:, :, None]
        carried = jnp.exp(cumulative[:, -1])[:, None, None] * carried + contrib
        return (carried, result)
    initial = jnp.zeros((MIXER_HEADS, P_SIZE, STATE), jnp.float32)
    unused_item, outputs = lax.scan(block_step, initial, (x_blocks, dt_blocks, b_blocks, c_blocks))
    return outputs.reshape(x_seq.shape[0], MIXER_HEADS, P_SIZE)

def reference(ssm_input, gate_input, state_proj, step_raw, decay_log, skip_gain, norm_gain, out_weight, latents, lengths):
    decay_rates = jnp.exp(decay_log)
    score_scale = 1.0 / math.sqrt(D)
    gain_heads = norm_gain.reshape(MIXER_HEADS, P_SIZE)

    def one_sequence(operands):
        ssm_seq, gate_seq, proj_seq, raw_seq, length = operands
        symbol_offset = jnp.arange(SEQUENCE_TOKENS, dtype=jnp.int32)
        is_valid = symbol_offset < length
        quantized_stride_width = jnp.where(is_valid[None, :], jax.nn.softplus(raw_seq), 0.0)
        tokens = ssm_seq.reshape(SEQUENCE_TOKENS, MIXER_HEADS, P_SIZE)
        forward_out = scan_sequence(tokens, quantized_stride_width[:MIXER_HEADS], proj_seq[:, :STATE], proj_seq[:, STATE:2 * STATE], decay_rates[0])
        backward_out = scan_sequence(tokens[::-1], quantized_stride_width[MIXER_HEADS:, ::-1], proj_seq[::-1, 2 * STATE:3 * STATE], proj_seq[::-1, 3 * STATE:], decay_rates[1])[::-1]
        mixed_out = forward_out + backward_out + skip_gain[None, :, None] * tokens.astype(jnp.float32)
        gated_out = mixed_out * jax.nn.silu(gate_seq.reshape(SEQUENCE_TOKENS, MIXER_HEADS, P_SIZE).astype(jnp.float32))
        mean_square = lax.optimization_barrier(jnp.mean(gated_out * gated_out, axis=2, keepdims=True))
        normed = (gated_out * lax.rsqrt(mean_square + 1e-05) * gain_heads[None]).astype(jnp.bfloat16).reshape(SEQUENCE_TOKENS, HP)
        encoded = jnp.dot(normed, out_weight, preferred_element_type=jnp.float32).astype(jnp.bfloat16)
        scores = jnp.dot(latents, encoded.T, preferred_element_type=jnp.float32) * score_scale
        top_score = lax.optimization_barrier(jnp.max(jnp.where(is_valid[None, :], scores, -1e+30), axis=1))
        prob_values = jnp.where(is_valid[None, :], jnp.exp(scores - top_score[:, None]), 0.0)
        weight_sum = lax.optimization_barrier(jnp.sum(prob_values, axis=1))
        weighted_sum = jnp.dot(prob_values.astype(jnp.bfloat16), encoded, preferred_element_type=jnp.float32)
        pooled = (weighted_sum / weight_sum[:, None]).astype(jnp.bfloat16)
        return (encoded, pooled)
    encoded, pooled = lax.map(one_sequence, (ssm_input, gate_input, state_proj, step_raw, lengths))
    return (encoded, pooled)
```

```python
import functools
import math

import jax
import jax.numpy as jnp
from jax import lax
from jax.experimental import pallas as pl
from jax.experimental.pallas import tpu as pltpu
from jax.sharding import PartitionSpec as P

CHUNK = 256
PAIR = 128
F32 = jnp.float32
BF16 = jnp.bfloat16


def dot(a, b, dims=((1,), (0,)), precision=None):
    return lax.dot_general(
        a, b, (dims, ((), ())), precision=precision, preferred_element_type=F32
    )


def column_of(row, size):
    eye = lax.broadcasted_iota(jnp.int32, (size, size), 0) == lax.broadcasted_iota(
        jnp.int32, (size, size), 1
    )
    return jnp.sum(jnp.where(eye, jnp.broadcast_to(row, (size, size)), 0.0), axis=1, keepdims=True)


def kernel(
    n,
    n_dp,
    lengths,
    skip,
    x_ref,
    gate_ref,
    proj_ref,
    raw_ref,
    decay_ref,
    gain_ref,
    w_ref,
    latents_ref,
    enc_ref,
    pooled_ref,
    w_all,
    own_state,
    own_decay,
    state_send,
    pair_in,
    chain_in,
    chain_out,
    leaf_in,
    incoming,
    head_out,
    factor,
    normed,
    sum_send,
    stat_send,
    sum_recv,
    stat_recv,
    pool,
    w_send_sem,
    w_fwd_sem,
    w_recv_sem,
    pair_send_sem,
    pair_recv_sem,
    chain_send_sem,
    chain_recv_sem,
    leaf_send_sem,
    leaf_recv_sem,
    sum_send_sem,
    sum_recv_sem,
    stat_send_sem,
    stat_recv_sem,
    pool_send_sem,
    pool_recv_sem,
):
    rows, width = x_ref.shape[1], x_ref.shape[2]
    heads = decay_ref.shape[1]
    head_size = width // heads
    state = proj_ref.shape[2] // 4
    chunks = width // CHUNK
    w_rows = w_ref.shape[0]
    me = lax.axis_index("seq")
    my_dp = lax.axis_index("dp")

    def remote(src, dst, send_sem, recv_sem, seq=None, dp=None):
        device_id = {"seq": seq} if dp is None else {"dp": dp}
        return pltpu.make_async_remote_copy(
            src_ref=src,
            dst_ref=dst,
            send_sem=send_sem,
            recv_sem=recv_sem,
            device_id=device_id,
            device_id_type=pl.DeviceIdType.MESH,
        )

    side = lax.rem(me, 2)
    place = me // 2
    places = n // 2
    partner = me + 1 - 2 * side
    node_dir = 1 - side
    along = jnp.where(side == 1, place, places - 1 - place)
    leaf_along = jnp.where(side == 1, places - 1 - place, place)
    following = lax.rem(me + 4 * side - 2 + n, n)
    core = lax.rem(my_dp, 2)
    dp_partner = my_dp + 1 - 2 * core

    barrier = pltpu.get_barrier_semaphore()
    for step in range(1, n):
        pl.semaphore_signal(
            barrier,
            inc=1,
            device_id={"seq": lax.rem(me + step, n)},
            device_id_type=pl.DeviceIdType.MESH,
        )
    pl.semaphore_signal(
        barrier, inc=1, device_id={"dp": dp_partner}, device_id_type=pl.DeviceIdType.MESH
    )
    for step in range(2, n_dp, 2):
        pl.semaphore_signal(
            barrier,
            inc=1,
            device_id={"dp": lax.rem(my_dp + step, n_dp)},
            device_id_type=pl.DeviceIdType.MESH,
        )
    pl.semaphore_wait(barrier, n - 1 + n_dp // 2)

    def w_slot(owner):
        return w_all.at[pl.ds(pl.multiple_of(owner * w_rows, w_rows), w_rows)]

    w_copies = []
    for step in range(2, n_dp, 2):
        w_copies.append(
            remote(
                w_ref,
                w_slot(my_dp),
                w_send_sem.at[step],
                w_recv_sem.at[step],
                dp=lax.rem(my_dp + step, n_dp),
            )
        )
    w_copies.append(
        remote(w_ref, w_slot(my_dp), w_send_sem.at[0], w_recv_sem.at[0], dp=dp_partner)
    )
    for copy in w_copies:
        copy.start()

    token = lax.broadcasted_iota(jnp.int32, (1, rows), 1)
    valid = (me * rows + token) < lengths[0]
    raw = raw_ref[0]
    softplus = jnp.maximum(raw, 0.0) + jnp.log1p(jnp.exp(-jnp.abs(raw)))
    dt = jnp.where(valid, softplus, 0.0)
    rates = jnp.exp(decay_ref[...])
    step_f, step_b = dt[:heads], dt[heads:]
    loss_f = -step_f * column_of(rates[0:1], heads)
    loss_b = -step_b * column_of(rates[1:2], heads)
    row_at = lax.broadcasted_iota(jnp.int32, (rows, rows), 0)
    col_at = lax.broadcasted_iota(jnp.int32, (rows, rows), 1)
    cum_f = dot(loss_f, jnp.where(row_at <= col_at, 1.0, 0.0), precision=lax.Precision.HIGHEST)
    cum_b = dot(loss_b, jnp.where(row_at >= col_at, 1.0, 0.0), precision=lax.Precision.HIGHEST)
    stacked = jnp.concatenate(
        [cum_f, cum_b, step_f, step_b, jnp.zeros((128 - 4 * heads, rows), F32)], axis=0
    )
    by_token = stacked.T
    col_f, col_b = by_token[:, :heads], by_token[:, heads : 2 * heads]
    dt_f, dt_b = by_token[:, 2 * heads : 3 * heads], by_token[:, 3 * heads : 4 * heads]
    tail_f = jnp.exp(col_f[rows - 1 : rows] - col_f) * dt_f
    tail_b = jnp.exp(col_b[0:1] - col_b) * dt_b
    grow_f, grow_b = jnp.exp(col_f), jnp.exp(col_b)

    head_row = lax.broadcasted_iota(jnp.int32, (heads, width), 0) * head_size
    head_lane = lax.broadcasted_iota(jnp.int32, (heads, width), 1)
    spread = jnp.where(
        (head_lane >= head_row) & (head_lane < head_row + head_size), 1.0, 0.0
    ).astype(BF16)

    def split(values):
        high = values.astype(BF16)
        return high, (values - high.astype(F32)).astype(BF16)

    def widen(parts, c):
        columns = spread[:, c * CHUNK : (c + 1) * CHUNK]
        return dot(parts[0], columns) + dot(parts[1], columns)

    proj = proj_ref[0]
    b_f, c_f = proj[:, :state], proj[:, state : 2 * state]
    b_b, c_b = proj[:, 2 * state : 3 * state], proj[:, 3 * state :]

    tails = (split(tail_f), split(tail_b))
    grows = (split(grow_f), split(grow_b))
    for c in range(chunks):
        columns = slice(c * CHUNK, (c + 1) * CHUNK)
        x_chunk = x_ref[0, :, columns].astype(F32)
        for d, b_d in ((0, b_f), (1, b_b)):
            scaled = (x_chunk * widen(tails[d], c)).astype(BF16)
            total = dot(b_d, scaled, ((0,), (0,)))
            grow = widen(grows[d], c)
            factor[d, :, columns] = grow
            decay = grow[rows - 1 : rows] if d == 0 else grow[0:1]
            own_state[d, c] = total
            own_decay[d, c] = jnp.broadcast_to(decay, (8, CHUNK))
            state_send[d, c, :state] = total.astype(BF16)
            high, low = split(decay)
            state_send[d, c, state:] = jnp.where(
                lax.broadcasted_iota(jnp.int32, (16, CHUNK), 0) == 0,
                high.astype(F32),
                jnp.where(
                    lax.broadcasted_iota(jnp.int32, (16, CHUNK), 0) == 1, low.astype(F32), 0.0
                ),
            ).astype(BF16)
        remote(
            state_send.at[side, c],
            pair_in.at[c],
            pair_send_sem.at[c],
            pair_recv_sem.at[c],
            seq=partner,
        ).start()

    gram_f = dot(c_f, b_f, ((1,), (1,)))
    gram_b = dot(c_b, b_b, ((1,), (1,)))
    earlier = col_at < row_at
    gram = jnp.where(earlier, gram_f, jnp.where(col_at == row_at, 0.0, gram_b))
    self_f = jnp.sum(c_f.astype(F32) * b_f.astype(F32), axis=1, keepdims=True)
    self_b = jnp.sum(c_b.astype(F32) * b_b.astype(F32), axis=1, keepdims=True)
    lane = lax.broadcasted_iota(jnp.int32, (rows, PAIR), 1)

    def own_part(first_pair, last_pair):
        for pair in range(first_pair, last_pair):
            columns = slice(pair * PAIR, (pair + 1) * PAIR)
            x_pair = x_ref[0, :, columns]
            result = None
            direct = None
            for k in range(PAIR // head_size):
                h = pair * (PAIR // head_size) + k
                gap = jnp.where(
                    earlier,
                    col_f[:, h : h + 1] - cum_f[h : h + 1],
                    col_b[:, h : h + 1] - cum_b[h : h + 1],
                )
                weight = jnp.where(earlier, step_f[h : h + 1], step_b[h : h + 1])
                mixing = (gram * jnp.exp(gap) * weight).astype(BF16)
                mine = (lane >= k * head_size) & (lane < (k + 1) * head_size)
                part = dot(mixing, jnp.where(mine, x_pair, jnp.zeros_like(x_pair)))
                own = self_f * dt_f[:, h : h + 1] + self_b * dt_b[:, h : h + 1] + skip[h]
                result = part if result is None else result + part
                own = jnp.broadcast_to(own, (rows, PAIR))
                direct = own if direct is None else jnp.where(mine, own, direct)
            head_out[:, columns] = result + direct * x_pair.astype(F32)

    own_part(0, width // PAIR)

    def chain_copy(c):
        return remote(
            chain_out.at[c],
            chain_in.at[c],
            chain_send_sem.at[c],
            chain_recv_sem.at[c],
            seq=following,
        )

    def leaf_copy(c):
        return remote(
            chain_in.at[c],
            leaf_in.at[c],
            leaf_send_sem.at[c],
            leaf_recv_sem.at[c],
            seq=partner,
        )

    def pair_copy(c):
        return remote(
            state_send.at[side, c],
            pair_in.at[c],
            pair_send_sem.at[c],
            pair_recv_sem.at[c],
            seq=partner,
        )

    @pl.when(along == 0)
    def _():
        chain_in[...] = jnp.zeros_like(chain_in)

    @pl.when(leaf_along == 0)
    def _():
        leaf_in[...] = jnp.zeros_like(leaf_in)

    for c in range(chunks):
        pair_copy(c).wait_recv()
        pair_state = pair_in[c, :state].astype(F32)
        pair_tail = pair_in[c, state:].astype(F32)
        pair_decay = pair_tail[0:1] + pair_tail[1:2]
        my_decay = own_decay[node_dir, c][0:1]

        @pl.when(along > 0)
        def _():
            chain_copy(c).wait_recv()
            leaf_copy(c).start()

        entering = pair_decay * chain_in[c].astype(F32) + pair_state
        incoming[node_dir, c] = entering.astype(BF16)

        @pl.when(along < places - 1)
        def _():
            chain_out[c] = (my_decay * entering + own_state[node_dir, c]).astype(BF16)
            chain_copy(c).start()

    w_all[pl.ds(pl.multiple_of(my_dp * w_rows, w_rows), w_rows)] = w_ref[...]
    forwards = []
    for i, step in enumerate(range(2, n_dp, 2)):
        w_copies[i].wait_recv()
        owner = lax.rem(my_dp + n_dp - step, n_dp)
        forward = remote(
            w_slot(owner),
            w_slot(owner),
            w_fwd_sem.at[step],
            w_recv_sem.at[step + 1],
            dp=dp_partner,
        )
        forward.start()
        forwards.append(forward)

    for c in range(chunks):
        columns = slice(c * CHUNK, (c + 1) * CHUNK)

        @pl.when(leaf_along > 0)
        def _():
            leaf_copy(c).wait_recv()

        incoming[side, c] = leaf_in[c]
        mixed = (
            head_out[:, columns]
            + dot(c_f, incoming[0, c]) * factor[0, :, columns]
            + dot(c_b, incoming[1, c]) * factor[1, :, columns]
        )
        gate = gate_ref[0, :, columns].astype(F32)
        gated = mixed * (gate / (1.0 + jnp.exp(-gate)))
        spread_chunk = spread[:, columns]
        square = split(gated * gated)
        mean = (
            dot(square[0], spread_chunk, ((1,), (1,))) + dot(square[1], spread_chunk, ((1,), (1,)))
        ) * (1.0 / head_size)
        scale = widen(split(lax.rsqrt(mean + 1e-05)), c)
        normed[:, columns] = (gated * scale * gain_ref[:, columns]).astype(BF16)

    w_copies[-1].wait_recv()
    for copy in forwards:
        copy.wait_recv()
    for c in range(chunks):
        columns = slice(c * CHUNK, (c + 1) * CHUNK)
        enc_ref[0, :, columns] = dot(normed[...], w_all[:, columns]).astype(BF16)

    encoded = enc_ref[0]
    scores = dot(latents_ref[...], encoded, ((1,), (1,))) * (1.0 / math.sqrt(encoded.shape[1]))
    top = jnp.max(jnp.where(valid, scores, -1e30), axis=1, keepdims=True)
    prob = jnp.where(valid, jnp.exp(scores - top), 0.0)
    weight_sum = jnp.sum(prob, axis=1, keepdims=True)
    queries = latents_ref.shape[0]
    share = queries // n
    half = lax.broadcasted_iota(jnp.int32, (queries, 128), 1) < 64
    stat_send[...] = jnp.where(half, top, weight_sum).reshape(n, share, 128)
    prob_low = prob.astype(BF16)
    for c in range(encoded.shape[1] // CHUNK):
        columns = slice(c * CHUNK, (c + 1) * CHUNK)
        part = dot(prob_low, encoded[:, columns])
        sum_send[:, :, columns] = part.reshape(n, share, CHUNK).astype(BF16)

    sum_copies, stat_copies = [], []
    for step in range(1, n):
        target = lax.rem(me + step, n)
        stat_copies.append(
            remote(
                stat_send.at[target],
                stat_recv.at[step],
                stat_send_sem.at[step],
                stat_recv_sem.at[step],
                seq=target,
            )
        )
        sum_copies.append(
            remote(
                sum_send.at[target],
                sum_recv.at[step],
                sum_send_sem.at[step],
                sum_recv_sem.at[step],
                seq=target,
            )
        )
    for copy in stat_copies:
        copy.start()
    for copy in sum_copies:
        copy.start()
    stat_recv[0] = stat_send[me]
    for copy in stat_copies:
        copy.wait_recv()
    tops = [stat_recv[step][:, 0:1] for step in range(n)]
    best = functools.reduce(jnp.maximum, tops)
    scales = [jnp.exp(t - best) for t in tops]
    whole = functools.reduce(
        jnp.add, [stat_recv[step][:, 64:65] * scales[step] for step in range(n)]
    )
    inverse = 1.0 / whole
    total = sum_send[me].astype(F32) * (scales[0] * inverse)
    for step in range(1, n):
        sum_copies[step - 1].wait_recv()
        total = total + sum_recv[step].astype(F32) * (scales[step] * inverse)
    pool[me] = total.astype(BF16)
    pool_copies = []
    for step in range(1, n):
        target = lax.rem(me + step, n)
        copy = remote(
            pool.at[me],
            pool.at[me],
            pool_send_sem.at[step],
            pool_recv_sem.at[step],
            seq=target,
        )
        copy.start()
        pool_copies.append(copy)
    for copy in pool_copies:
        copy.wait_recv()
    pooled_ref[0] = pool[...].reshape(queries, pool.shape[2])

    for copy in w_copies + forwards + sum_copies + stat_copies + pool_copies:
        copy.wait_send()
    for c in range(chunks):
        pair_copy(c).wait_send()

        @pl.when(along < places - 1)
        def _():
            chain_copy(c).wait_send()

        @pl.when(along > 0)
        def _():
            leaf_copy(c).wait_send()


def body(
    n,
    n_dp,
    ssm_input,
    gate_input,
    state_proj,
    step_raw,
    decay_log,
    skip_gain,
    norm_gain,
    out_weight,
    latents,
    lengths,
):
    rows, width = ssm_input.shape[1], ssm_input.shape[2]
    model = out_weight.shape[1]
    state = state_proj.shape[2] // 4
    queries = latents.shape[0]
    share = queries // n
    chunks = width // CHUNK
    vmem = pl.BlockSpec(memory_space=pltpu.VMEM)
    smem = pl.BlockSpec(memory_space=pltpu.SMEM)
    dma = pltpu.SemaphoreType.DMA
    return pl.pallas_call(
        functools.partial(kernel, n, n_dp),
        out_shape=(
            jax.ShapeDtypeStruct((1, rows, model), BF16),
            jax.ShapeDtypeStruct((1, queries, model), BF16),
        ),
        in_specs=[smem, smem] + [vmem] * 8,
        out_specs=(vmem, vmem),
        scratch_shapes=[
            pltpu.VMEM((width, model), BF16),
            pltpu.VMEM((2, chunks, state, CHUNK), F32),
            pltpu.VMEM((2, chunks, 8, CHUNK), F32),
            pltpu.VMEM((2, chunks, state + 16, CHUNK), BF16),
            pltpu.VMEM((chunks, state + 16, CHUNK), BF16),
            pltpu.VMEM((chunks, state, CHUNK), BF16),
            pltpu.VMEM((chunks, state, CHUNK), BF16),
            pltpu.VMEM((chunks, state, CHUNK), BF16),
            pltpu.VMEM((2, chunks, state, CHUNK), BF16),
            pltpu.VMEM((rows, width), F32),
            pltpu.VMEM((2, rows, width), F32),
            pltpu.VMEM((rows, width), BF16),
            pltpu.VMEM((n, share, model), BF16),
            pltpu.VMEM((n, share, 128), F32),
            pltpu.VMEM((n, share, model), BF16),
            pltpu.VMEM((n, share, 128), F32),
            pltpu.VMEM((n, share, model), BF16),
            dma((n_dp,)),
            dma((n_dp,)),
            dma((n_dp,)),
            dma((chunks,)),
            dma((chunks,)),
            dma((chunks,)),
            dma((chunks,)),
            dma((chunks,)),
            dma((chunks,)),
            dma((n,)),
            dma((n,)),
            dma((n,)),
            dma((n,)),
            dma((n,)),
            dma((n,)),
        ],
        compiler_params=pltpu.CompilerParams(
            collective_id=0, has_side_effects=True, vmem_limit_bytes=48 * 1024 * 1024
        ),
    )(
        lengths,
        skip_gain,
        ssm_input,
        gate_input,
        state_proj,
        step_raw,
        decay_log,
        norm_gain.reshape(1, width),
        out_weight,
        latents,
    )


def solution(mesh):
    in_specs = (
        P("dp", "seq", None),
        P("dp", "seq", None),
        P("dp", "seq", None),
        P("dp", None, "seq"),
        P(),
        P(),
        P(),
        P("dp", None),
        P(),
        P("dp"),
    )
    out_specs = (P("dp", "seq", None), P("dp", None, None))
    return jax.shard_map(
        functools.partial(body, mesh.shape["seq"], mesh.shape["dp"]),
        mesh=mesh,
        in_specs=in_specs,
        out_specs=out_specs,
        check_vma=False,
    )
```

```python
import functools
import math

import jax
import jax.numpy as jnp
from jax import lax
from jax.experimental import pallas as pl
from jax.experimental.pallas import tpu as pltpu
from jax.sharding import PartitionSpec as P

CHUNK = 256
PAIR = 128
F32 = jnp.float32
BF16 = jnp.bfloat16


def dot(a, b, dims=((1,), (0,)), precision=None):
    return lax.dot_general(
        a, b, (dims, ((), ())), precision=precision, preferred_element_type=F32
    )


def column_of(row, size):
    eye = lax.broadcasted_iota(jnp.int32, (size, size), 0) == lax.broadcasted_iota(
        jnp.int32, (size, size), 1
    )
    return jnp.sum(jnp.where(eye, jnp.broadcast_to(row, (size, size)), 0.0), axis=1, keepdims=True)


def kernel(
    n,
    n_dp,
    lengths,
    skip,
    x_hbm,
    gate_hbm,
    proj_hbm,
    raw_hbm,
    decay_hbm,
    gain_hbm,
    w_ref,
    latents_hbm,
    enc_ref,
    pooled_ref,
    x_ref,
    gate_ref,
    proj_ref,
    raw_ref,
    decay_ref,
    gain_ref,
    latents_ref,
    silu,
    load_sem,
    w_all,
    own_state,
    own_decay,
    state_send,
    pair_in,
    chain_in,
    chain_out,
    leaf_in,
    incoming,
    head_out,
    factor,
    normed,
    sum_send,
    stat_send,
    sum_recv,
    stat_recv,
    pool,
    w_send_sem,
    w_fwd_sem,
    w_recv_sem,
    pair_send_sem,
    pair_recv_sem,
    chain_send_sem,
    chain_recv_sem,
    leaf_send_sem,
    leaf_recv_sem,
    sum_send_sem,
    sum_recv_sem,
    stat_send_sem,
    stat_recv_sem,
    pool_send_sem,
    pool_recv_sem,
):
    rows, width = x_ref.shape[1], x_ref.shape[2]
    heads = decay_ref.shape[1]
    head_size = width // heads
    state = proj_ref.shape[2] // 4
    chunks = width // CHUNK
    w_rows = w_ref.shape[0]
    me = lax.axis_index("seq")
    my_dp = lax.axis_index("dp")

    def remote(src, dst, send_sem, recv_sem, seq=None, dp=None):
        device_id = {"seq": seq} if dp is None else {"dp": dp}
        return pltpu.make_async_remote_copy(
            src_ref=src,
            dst_ref=dst,
            send_sem=send_sem,
            recv_sem=recv_sem,
            device_id=device_id,
            device_id_type=pl.DeviceIdType.MESH,
        )

    side = lax.rem(me, 2)
    place = me // 2
    places = n // 2
    partner = me + 1 - 2 * side
    node_dir = 1 - side
    along = jnp.where(side == 1, place, places - 1 - place)
    leaf_along = jnp.where(side == 1, places - 1 - place, place)
    following = lax.rem(me + 4 * side - 2 + n, n)
    core = lax.rem(my_dp, 2)
    dp_partner = my_dp + 1 - 2 * core

    loads = [
        pltpu.make_async_copy(source, target, load_sem.at[i])
        for i, (source, target) in enumerate(
            (
                (raw_hbm, raw_ref),
                (decay_hbm, decay_ref),
                (proj_hbm, proj_ref),
                (x_hbm, x_ref),
                (gate_hbm, gate_ref),
                (gain_hbm, gain_ref),
                (latents_hbm, latents_ref),
                (w_ref, w_all.at[pl.ds(pl.multiple_of(my_dp * w_rows, w_rows), w_rows)]),
            )
        )
    ]
    for load in loads:
        load.start()

    barrier = pltpu.get_barrier_semaphore()
    for step in range(1, n):
        pl.semaphore_signal(
            barrier,
            inc=1,
            device_id={"seq": lax.rem(me + step, n)},
            device_id_type=pl.DeviceIdType.MESH,
        )
    pl.semaphore_signal(
        barrier, inc=1, device_id={"dp": dp_partner}, device_id_type=pl.DeviceIdType.MESH
    )
    for step in range(2, n_dp, 2):
        pl.semaphore_signal(
            barrier,
            inc=1,
            device_id={"dp": lax.rem(my_dp + step, n_dp)},
            device_id_type=pl.DeviceIdType.MESH,
        )
    pl.semaphore_wait(barrier, n - 1 + n_dp // 2)

    def w_slot(owner):
        return w_all.at[pl.ds(pl.multiple_of(owner * w_rows, w_rows), w_rows)]

    w_copies = []
    for step in range(2, n_dp, 2):
        w_copies.append(
            remote(
                w_ref,
                w_slot(my_dp),
                w_send_sem.at[step],
                w_recv_sem.at[step],
                dp=lax.rem(my_dp + step, n_dp),
            )
        )
    w_copies.append(
        remote(w_ref, w_slot(my_dp), w_send_sem.at[0], w_recv_sem.at[0], dp=dp_partner)
    )
    for copy in w_copies:
        copy.start()

    for load in loads[:4]:
        load.wait()

    token = lax.broadcasted_iota(jnp.int32, (1, rows), 1)
    valid = (me * rows + token) < lengths[0]
    raw = raw_ref[0]
    softplus = jnp.maximum(raw, 0.0) + jnp.log1p(jnp.exp(-jnp.abs(raw)))
    dt = jnp.where(valid, softplus, 0.0)
    rates = jnp.exp(decay_ref[...])
    step_f, step_b = dt[:heads], dt[heads:]
    loss_f = -step_f * column_of(rates[0:1], heads)
    loss_b = -step_b * column_of(rates[1:2], heads)
    row_at = lax.broadcasted_iota(jnp.int32, (rows, rows), 0)
    col_at = lax.broadcasted_iota(jnp.int32, (rows, rows), 1)
    cum_f = dot(loss_f, jnp.where(row_at <= col_at, 1.0, 0.0), precision=lax.Precision.HIGHEST)
    cum_b = dot(loss_b, jnp.where(row_at >= col_at, 1.0, 0.0), precision=lax.Precision.HIGHEST)
    stacked = jnp.concatenate(
        [cum_f, cum_b, step_f, step_b, jnp.zeros((128 - 4 * heads, rows), F32)], axis=0
    )
    by_token = stacked.T
    col_f, col_b = by_token[:, :heads], by_token[:, heads : 2 * heads]
    dt_f, dt_b = by_token[:, 2 * heads : 3 * heads], by_token[:, 3 * heads : 4 * heads]
    tail_f = jnp.exp(col_f[rows - 1 : rows] - col_f) * dt_f
    tail_b = jnp.exp(col_b[0:1] - col_b) * dt_b
    grow_f, grow_b = jnp.exp(col_f), jnp.exp(col_b)

    head_row = lax.broadcasted_iota(jnp.int32, (heads, width), 0) * head_size
    head_lane = lax.broadcasted_iota(jnp.int32, (heads, width), 1)
    spread = jnp.where(
        (head_lane >= head_row) & (head_lane < head_row + head_size), 1.0, 0.0
    ).astype(BF16)

    def split(values):
        high = values.astype(BF16)
        return high, (values - high.astype(F32)).astype(BF16)

    def widen(parts, c):
        columns = spread[:, c * CHUNK : (c + 1) * CHUNK]
        return dot(parts[0], columns) + dot(parts[1], columns)

    proj = proj_ref[0]
    b_f, c_f = proj[:, :state], proj[:, state : 2 * state]
    b_b, c_b = proj[:, 2 * state : 3 * state], proj[:, 3 * state :]

    tails = (split(tail_f), split(tail_b))
    grows = (split(grow_f), split(grow_b))
    ends = (
        split(jnp.broadcast_to(grow_f[rows - 1 : rows], (8, heads))),
        split(jnp.broadcast_to(grow_b[0:1], (8, heads))),
    )
    tail_row = lax.broadcasted_iota(jnp.int32, (16, CHUNK), 0)
    for c in range(chunks):
        columns = slice(c * CHUNK, (c + 1) * CHUNK)
        x_chunk = x_ref[0, :, columns].astype(F32)
        for d, b_d in ((0, b_f), (1, b_b)):
            scaled = (x_chunk * widen(tails[d], c)).astype(BF16)
            total = dot(b_d, scaled, ((0,), (0,)))
            decay = widen(ends[d], c)
            own_state[d, c] = total
            own_decay[d, c] = decay
            state_send[d, c, :state] = total.astype(BF16)
            high, low = split(decay[0:1])
            state_send[d, c, state:] = jnp.where(
                tail_row == 0,
                high.astype(F32),
                jnp.where(tail_row == 1, low.astype(F32), 0.0),
            ).astype(BF16)
        remote(
            state_send.at[side, c],
            pair_in.at[c],
            pair_send_sem.at[c],
            pair_recv_sem.at[c],
            seq=partner,
        ).start()

    gram_f = dot(c_f, b_f, ((1,), (1,)))
    gram_b = dot(c_b, b_b, ((1,), (1,)))
    earlier = col_at < row_at
    gram = jnp.where(earlier, gram_f, jnp.where(col_at == row_at, 0.0, gram_b))
    self_f = jnp.sum(c_f.astype(F32) * b_f.astype(F32), axis=1, keepdims=True)
    self_b = jnp.sum(c_b.astype(F32) * b_b.astype(F32), axis=1, keepdims=True)
    lane = lax.broadcasted_iota(jnp.int32, (rows, PAIR), 1)

    def own_part(first_pair, last_pair):
        for pair in range(first_pair, last_pair):
            columns = slice(pair * PAIR, (pair + 1) * PAIR)
            x_pair = x_ref[0, :, columns]
            result = None
            direct = None
            for k in range(PAIR // head_size):
                h = pair * (PAIR // head_size) + k
                gap = jnp.where(
                    earlier,
                    col_f[:, h : h + 1] - cum_f[h : h + 1],
                    col_b[:, h : h + 1] - cum_b[h : h + 1],
                )
                weight = jnp.where(earlier, step_f[h : h + 1], step_b[h : h + 1])
                mixing = (gram * jnp.exp(gap) * weight).astype(BF16)
                mine = (lane >= k * head_size) & (lane < (k + 1) * head_size)
                part = dot(mixing, jnp.where(mine, x_pair, jnp.zeros_like(x_pair)))
                own = self_f * dt_f[:, h : h + 1] + self_b * dt_b[:, h : h + 1] + skip[h]
                result = part if result is None else result + part
                own = jnp.broadcast_to(own, (rows, PAIR))
                direct = own if direct is None else jnp.where(mine, own, direct)
            head_out[:, columns] = result + direct * x_pair.astype(F32)

    pairs = width // PAIR
    own_part(0, pairs // 2)

    def chain_copy(c):
        return remote(
            chain_out.at[c],
            chain_in.at[c],
            chain_send_sem.at[c],
            chain_recv_sem.at[c],
            seq=following,
        )

    def leaf_copy(c):
        return remote(
            chain_in.at[c],
            leaf_in.at[c],
            leaf_send_sem.at[c],
            leaf_recv_sem.at[c],
            seq=partner,
        )

    def pair_copy(c):
        return remote(
            state_send.at[side, c],
            pair_in.at[c],
            pair_send_sem.at[c],
            pair_recv_sem.at[c],
            seq=partner,
        )

    @pl.when(along == 0)
    def _():
        chain_in[...] = jnp.zeros_like(chain_in)

    @pl.when(leaf_along == 0)
    def _():
        leaf_in[...] = jnp.zeros_like(leaf_in)

    for c in range(chunks):
        pair_copy(c).wait_recv()
        pair_state = pair_in[c, :state].astype(F32)
        pair_tail = pair_in[c, state:].astype(F32)
        pair_decay = pair_tail[0:1] + pair_tail[1:2]
        my_decay = own_decay[node_dir, c][0:1]

        @pl.when(along > 0)
        def _():
            chain_copy(c).wait_recv()
            leaf_copy(c).start()

        entering = pair_decay * chain_in[c].astype(F32) + pair_state
        incoming[node_dir, c] = entering.astype(BF16)

        @pl.when(along < places - 1)
        def _():
            chain_out[c] = (my_decay * entering + own_state[node_dir, c]).astype(BF16)
            chain_copy(c).start()

    own_part(pairs // 2, pairs)
    for load in loads[4:]:
        load.wait()
    for c in range(chunks):
        columns = slice(c * CHUNK, (c + 1) * CHUNK)
        for d in range(2):
            factor[d, :, columns] = widen(grows[d], c)
        gate = gate_ref[0, :, columns].astype(F32)
        silu[:, columns] = gate / (1.0 + jnp.exp(-gate))

    forwards = []
    for i, step in enumerate(range(2, n_dp, 2)):
        w_copies[i].wait_recv()
        owner = lax.rem(my_dp + n_dp - step, n_dp)
        forward = remote(
            w_slot(owner),
            w_slot(owner),
            w_fwd_sem.at[step],
            w_recv_sem.at[step + 1],
            dp=dp_partner,
        )
        forward.start()
        forwards.append(forward)

    for c in range(chunks):
        columns = slice(c * CHUNK, (c + 1) * CHUNK)

        @pl.when(leaf_along > 0)
        def _():
            leaf_copy(c).wait_recv()

        incoming[side, c] = leaf_in[c]
        mixed = (
            head_out[:, columns]
            + dot(c_f, incoming[0, c]) * factor[0, :, columns]
            + dot(c_b, incoming[1, c]) * factor[1, :, columns]
        )
        gated = mixed * silu[:, columns]
        spread_chunk = spread[:, columns]
        square = split(gated * gated)
        mean = (
            dot(square[0], spread_chunk, ((1,), (1,))) + dot(square[1], spread_chunk, ((1,), (1,)))
        ) * (1.0 / head_size)
        scale = widen(split(lax.rsqrt(mean + 1e-05)), c)
        normed[:, columns] = (gated * scale * gain_ref[:, columns]).astype(BF16)

    w_copies[-1].wait_recv()
    for copy in forwards:
        copy.wait_recv()
    for c in range(chunks):
        columns = slice(c * CHUNK, (c + 1) * CHUNK)
        enc_ref[0, :, columns] = dot(normed[...], w_all[:, columns]).astype(BF16)

    encoded = enc_ref[0]
    scores = dot(latents_ref[...], encoded, ((1,), (1,))) * (1.0 / math.sqrt(encoded.shape[1]))
    top = jnp.max(jnp.where(valid, scores, -1e30), axis=1, keepdims=True)
    prob = jnp.where(valid, jnp.exp(scores - top), 0.0)
    weight_sum = jnp.sum(prob, axis=1, keepdims=True)
    queries = latents_ref.shape[0]
    share = queries // n
    half = lax.broadcasted_iota(jnp.int32, (queries, 128), 1) < 64
    stat_send[...] = jnp.where(half, top, weight_sum).reshape(n, share, 128)
    prob_low = prob.astype(BF16)
    for c in range(encoded.shape[1] // CHUNK):
        columns = slice(c * CHUNK, (c + 1) * CHUNK)
        part = dot(prob_low, encoded[:, columns])
        sum_send[:, :, columns] = part.reshape(n, share, CHUNK).astype(BF16)

    sum_copies, stat_copies = [], []
    for step in range(1, n):
        target = lax.rem(me + step, n)
        stat_copies.append(
            remote(
                stat_send.at[target],
                stat_recv.at[step],
                stat_send_sem.at[step],
                stat_recv_sem.at[step],
                seq=target,
            )
        )
        sum_copies.append(
            remote(
                sum_send.at[target],
                sum_recv.at[step],
                sum_send_sem.at[step],
                sum_recv_sem.at[step],
                seq=target,
            )
        )
    for copy in stat_copies:
        copy.start()
    for copy in sum_copies:
        copy.start()
    stat_recv[0] = stat_send[me]
    for copy in stat_copies:
        copy.wait_recv()
    tops = [stat_recv[step][:, 0:1] for step in range(n)]
    best = functools.reduce(jnp.maximum, tops)
    scales = [jnp.exp(t - best) for t in tops]
    whole = functools.reduce(
        jnp.add, [stat_recv[step][:, 64:65] * scales[step] for step in range(n)]
    )
    inverse = 1.0 / whole
    total = sum_send[me].astype(F32) * (scales[0] * inverse)
    for step in range(1, n):
        sum_copies[step - 1].wait_recv()
        total = total + sum_recv[step].astype(F32) * (scales[step] * inverse)
    pool[me] = total.astype(BF16)
    pool_copies = []
    for step in range(1, n):
        target = lax.rem(me + step, n)
        copy = remote(
            pool.at[me],
            pool.at[me],
            pool_send_sem.at[step],
            pool_recv_sem.at[step],
            seq=target,
        )
        copy.start()
        pool_copies.append(copy)
    for copy in pool_copies:
        copy.wait_recv()
    pooled_ref[0] = pool[...].reshape(queries, pool.shape[2])

    for copy in w_copies + forwards + sum_copies + stat_copies + pool_copies:
        copy.wait_send()
    for c in range(chunks):
        pair_copy(c).wait_send()

        @pl.when(along < places - 1)
        def _():
            chain_copy(c).wait_send()

        @pl.when(along > 0)
        def _():
            leaf_copy(c).wait_send()


def body(
    n,
    n_dp,
    ssm_input,
    gate_input,
    state_proj,
    step_raw,
    decay_log,
    skip_gain,
    norm_gain,
    out_weight,
    latents,
    lengths,
):
    rows, width = ssm_input.shape[1], ssm_input.shape[2]
    model = out_weight.shape[1]
    state = state_proj.shape[2] // 4
    queries = latents.shape[0]
    share = queries // n
    chunks = width // CHUNK
    vmem = pl.BlockSpec(memory_space=pltpu.VMEM)
    smem = pl.BlockSpec(memory_space=pltpu.SMEM)
    dma = pltpu.SemaphoreType.DMA
    return pl.pallas_call(
        functools.partial(kernel, n, n_dp),
        out_shape=(
            jax.ShapeDtypeStruct((1, rows, model), BF16),
            jax.ShapeDtypeStruct((1, queries, model), BF16),
        ),
        in_specs=[smem, smem] + [pl.BlockSpec(memory_space=pltpu.HBM)] * 8,
        out_specs=(vmem, vmem),
        scratch_shapes=[
            pltpu.VMEM(ssm_input.shape, BF16),
            pltpu.VMEM(gate_input.shape, BF16),
            pltpu.VMEM(state_proj.shape, BF16),
            pltpu.VMEM(step_raw.shape, F32),
            pltpu.VMEM(decay_log.shape, F32),
            pltpu.VMEM((1, width), F32),
            pltpu.VMEM(latents.shape, BF16),
            pltpu.VMEM((rows, width), F32),
            dma((8,)),
            pltpu.VMEM((width, model), BF16),
            pltpu.VMEM((2, chunks, state, CHUNK), F32),
            pltpu.VMEM((2, chunks, 8, CHUNK), F32),
            pltpu.VMEM((2, chunks, state + 16, CHUNK), BF16),
            pltpu.VMEM((chunks, state + 16, CHUNK), BF16),
            pltpu.VMEM((chunks, state, CHUNK), BF16),
            pltpu.VMEM((chunks, state, CHUNK), BF16),
            pltpu.VMEM((chunks, state, CHUNK), BF16),
            pltpu.VMEM((2, chunks, state, CHUNK), BF16),
            pltpu.VMEM((rows, width), F32),
            pltpu.VMEM((2, rows, width), F32),
            pltpu.VMEM((rows, width), BF16),
            pltpu.VMEM((n, share, model), BF16),
            pltpu.VMEM((n, share, 128), F32),
            pltpu.VMEM((n, share, model), BF16),
            pltpu.VMEM((n, share, 128), F32),
            pltpu.VMEM((n, share, model), BF16),
            dma((n_dp,)),
            dma((n_dp,)),
            dma((n_dp,)),
            dma((chunks,)),
            dma((chunks,)),
            dma((chunks,)),
            dma((chunks,)),
            dma((chunks,)),
            dma((chunks,)),
            dma((n,)),
            dma((n,)),
            dma((n,)),
            dma((n,)),
            dma((n,)),
            dma((n,)),
        ],
        compiler_params=pltpu.CompilerParams(
            collective_id=0, has_side_effects=True, vmem_limit_bytes=48 * 1024 * 1024
        ),
    )(
        lengths,
        skip_gain,
        ssm_input,
        gate_input,
        state_proj,
        step_raw,
        decay_log,
        norm_gain.reshape(1, width),
        out_weight,
        latents,
    )


def solution(mesh):
    in_specs = (
        P("dp", "seq", None),
        P("dp", "seq", None),
        P("dp", "seq", None),
        P("dp", None, "seq"),
        P(),
        P(),
        P(),
        P("dp", None),
        P(),
        P("dp"),
    )
    out_specs = (P("dp", "seq", None), P("dp", None, None))
    return jax.shard_map(
        functools.partial(body, mesh.shape["seq"], mesh.shape["dp"]),
        mesh=mesh,
        in_specs=in_specs,
        out_specs=out_specs,
        check_vma=False,
    )
```

```python
import functools
import math

import jax
import jax.numpy as jnp
from jax import lax
from jax.experimental import pallas as pl
from jax.experimental.pallas import tpu as pltpu
from jax.sharding import PartitionSpec as P

CHUNK = 256
PAIR = 128
F32 = jnp.float32
BF16 = jnp.bfloat16


def dot(a, b, dims=((1,), (0,)), precision=None):
    return lax.dot_general(
        a, b, (dims, ((), ())), precision=precision, preferred_element_type=F32
    )


def column_of(row, size):
    eye = lax.broadcasted_iota(jnp.int32, (size, size), 0) == lax.broadcasted_iota(
        jnp.int32, (size, size), 1
    )
    return jnp.sum(jnp.where(eye, jnp.broadcast_to(row, (size, size)), 0.0), axis=1, keepdims=True)


def kernel(
    n,
    n_dp,
    lengths,
    skip,
    x_hbm,
    gate_hbm,
    proj_hbm,
    raw_hbm,
    decay_hbm,
    gain_hbm,
    w_ref,
    latents_hbm,
    enc_ref,
    pooled_ref,
    x_ref,
    gate_ref,
    proj_ref,
    raw_ref,
    decay_ref,
    gain_ref,
    latents_ref,
    silu,
    load_sem,
    w_all,
    own_state,
    own_decay,
    state_send,
    pair_in,
    chain_in,
    chain_out,
    leaf_in,
    incoming,
    head_out,
    factor,
    normed,
    sum_send,
    sum_pair,
    sum_both,
    sum_recv,
    pool,
    w_send_sem,
    w_fwd_sem,
    w_recv_sem,
    pair_send_sem,
    pair_recv_sem,
    chain_send_sem,
    chain_recv_sem,
    leaf_send_sem,
    leaf_recv_sem,
    sum_send_sem,
    sum_recv_sem,
    stat_send_sem,
    stat_recv_sem,
    pool_send_sem,
    pool_recv_sem,
    hand_send_sem,
    hand_recv_sem,
):
    rows, width = x_ref.shape[1], x_ref.shape[2]
    heads = decay_ref.shape[1]
    head_size = width // heads
    state = proj_ref.shape[2] // 4
    chunks = width // CHUNK
    w_rows = w_ref.shape[0]
    me = lax.axis_index("seq")
    my_dp = lax.axis_index("dp")

    def remote(src, dst, send_sem, recv_sem, seq=None, dp=None):
        device_id = {"seq": seq} if dp is None else {"dp": dp}
        return pltpu.make_async_remote_copy(
            src_ref=src,
            dst_ref=dst,
            send_sem=send_sem,
            recv_sem=recv_sem,
            device_id=device_id,
            device_id_type=pl.DeviceIdType.MESH,
        )

    side = lax.rem(me, 2)
    place = me // 2
    places = n // 2
    partner = me + 1 - 2 * side
    node_dir = 1 - side
    along = jnp.where(side == 1, place, places - 1 - place)
    leaf_along = jnp.where(side == 1, places - 1 - place, place)
    following = lax.rem(me + 4 * side - 2 + n, n)
    core = lax.rem(my_dp, 2)
    dp_partner = my_dp + 1 - 2 * core

    loads = [
        pltpu.make_async_copy(source, target, load_sem.at[i])
        for i, (source, target) in enumerate(
            (
                (raw_hbm, raw_ref),
                (decay_hbm, decay_ref),
                (proj_hbm, proj_ref),
                (x_hbm, x_ref),
                (gate_hbm, gate_ref),
                (gain_hbm, gain_ref),
                (latents_hbm, latents_ref),
                (w_ref, w_all.at[pl.ds(pl.multiple_of(my_dp * w_rows, w_rows), w_rows)]),
            )
        )
    ]
    for load in loads:
        load.start()

    barrier = pltpu.get_barrier_semaphore()
    for neighbour in [partner] + [
        2 * lax.rem(place + step, places) + side for step in range(1, places)
    ]:
        pl.semaphore_signal(
            barrier,
            inc=1,
            device_id={"seq": neighbour},
            device_id_type=pl.DeviceIdType.MESH,
        )
    pl.semaphore_signal(
        barrier, inc=1, device_id={"dp": dp_partner}, device_id_type=pl.DeviceIdType.MESH
    )
    for step in range(2, n_dp, 2):
        pl.semaphore_signal(
            barrier,
            inc=1,
            device_id={"dp": lax.rem(my_dp + step, n_dp)},
            device_id_type=pl.DeviceIdType.MESH,
        )
    pl.semaphore_wait(barrier, places + n_dp // 2)

    def w_slot(owner):
        return w_all.at[pl.ds(pl.multiple_of(owner * w_rows, w_rows), w_rows)]

    w_copies = []
    for step in range(2, n_dp, 2):
        w_copies.append(
            remote(
                w_ref,
                w_slot(my_dp),
                w_send_sem.at[step],
                w_recv_sem.at[step],
                dp=lax.rem(my_dp + step, n_dp),
            )
        )
    w_copies.append(
        remote(w_ref, w_slot(my_dp), w_send_sem.at[0], w_recv_sem.at[0], dp=dp_partner)
    )
    for copy in w_copies:
        copy.start()

    for load in loads[:4]:
        load.wait()

    token = lax.broadcasted_iota(jnp.int32, (1, rows), 1)
    valid = (me * rows + token) < lengths[0]
    raw = raw_ref[0]
    softplus = jnp.maximum(raw, 0.0) + jnp.log1p(jnp.exp(-jnp.abs(raw)))
    dt = jnp.where(valid, softplus, 0.0)
    rates = jnp.exp(decay_ref[...])
    step_f, step_b = dt[:heads], dt[heads:]
    loss_f = -step_f * column_of(rates[0:1], heads)
    loss_b = -step_b * column_of(rates[1:2], heads)
    row_at = lax.broadcasted_iota(jnp.int32, (rows, rows), 0)
    col_at = lax.broadcasted_iota(jnp.int32, (rows, rows), 1)
    cum_f = dot(loss_f, jnp.where(row_at <= col_at, 1.0, 0.0), precision=lax.Precision.HIGHEST)
    cum_b = dot(loss_b, jnp.where(row_at >= col_at, 1.0, 0.0), precision=lax.Precision.HIGHEST)
    stacked = jnp.concatenate(
        [cum_f, cum_b, step_f, step_b, jnp.zeros((128 - 4 * heads, rows), F32)], axis=0
    )
    by_token = stacked.T
    col_f, col_b = by_token[:, :heads], by_token[:, heads : 2 * heads]
    dt_f, dt_b = by_token[:, 2 * heads : 3 * heads], by_token[:, 3 * heads : 4 * heads]
    tail_f = jnp.exp(col_f[rows - 1 : rows] - col_f) * dt_f
    tail_b = jnp.exp(col_b[0:1] - col_b) * dt_b
    grow_f, grow_b = jnp.exp(col_f), jnp.exp(col_b)

    head_row = lax.broadcasted_iota(jnp.int32, (heads, width), 0) * head_size
    head_lane = lax.broadcasted_iota(jnp.int32, (heads, width), 1)
    spread = jnp.where(
        (head_lane >= head_row) & (head_lane < head_row + head_size), 1.0, 0.0
    ).astype(BF16)

    def split(values):
        high = values.astype(BF16)
        return high, (values - high.astype(F32)).astype(BF16)

    def widen(parts, c):
        columns = spread[:, c * CHUNK : (c + 1) * CHUNK]
        return dot(parts[0], columns) + dot(parts[1], columns)

    proj = proj_ref[0]
    b_f, c_f = proj[:, :state], proj[:, state : 2 * state]
    b_b, c_b = proj[:, 2 * state : 3 * state], proj[:, 3 * state :]

    tails = (split(tail_f), split(tail_b))
    grows = (split(grow_f), split(grow_b))
    ends = (
        split(jnp.broadcast_to(grow_f[rows - 1 : rows], (8, heads))),
        split(jnp.broadcast_to(grow_b[0:1], (8, heads))),
    )
    tail_row = lax.broadcasted_iota(jnp.int32, (16, CHUNK), 0)
    for c in range(chunks):
        columns = slice(c * CHUNK, (c + 1) * CHUNK)
        x_chunk = x_ref[0, :, columns].astype(F32)
        for d, b_d in ((0, b_f), (1, b_b)):
            scaled = (x_chunk * widen(tails[d], c)).astype(BF16)
            total = dot(b_d, scaled, ((0,), (0,)))
            decay = widen(ends[d], c)
            own_state[d, c] = total
            own_decay[d, c] = decay
            state_send[d, c, :state] = total.astype(BF16)
            high, low = split(decay[0:1])
            state_send[d, c, state:] = jnp.where(
                tail_row == 0,
                high.astype(F32),
                jnp.where(tail_row == 1, low.astype(F32), 0.0),
            ).astype(BF16)
        remote(
            state_send.at[side, c],
            pair_in.at[c],
            pair_send_sem.at[c],
            pair_recv_sem.at[c],
            seq=partner,
        ).start()

    gram_f = dot(c_f, b_f, ((1,), (1,)))
    gram_b = dot(c_b, b_b, ((1,), (1,)))
    earlier = col_at < row_at
    gram = jnp.where(earlier, gram_f, jnp.where(col_at == row_at, 0.0, gram_b))
    self_f = jnp.sum(c_f.astype(F32) * b_f.astype(F32), axis=1, keepdims=True)
    self_b = jnp.sum(c_b.astype(F32) * b_b.astype(F32), axis=1, keepdims=True)
    lane = lax.broadcasted_iota(jnp.int32, (rows, PAIR), 1)

    def own_part(first_pair, last_pair):
        for pair in range(first_pair, last_pair):
            columns = slice(pair * PAIR, (pair + 1) * PAIR)
            x_pair = x_ref[0, :, columns]
            result = None
            direct = None
            for k in range(PAIR // head_size):
                h = pair * (PAIR // head_size) + k
                gap = jnp.where(
                    earlier,
                    col_f[:, h : h + 1] - cum_f[h : h + 1],
                    col_b[:, h : h + 1] - cum_b[h : h + 1],
                )
                weight = jnp.where(earlier, step_f[h : h + 1], step_b[h : h + 1])
                mixing = (gram * jnp.exp(gap) * weight).astype(BF16)
                mine = (lane >= k * head_size) & (lane < (k + 1) * head_size)
                part = dot(mixing, jnp.where(mine, x_pair, jnp.zeros_like(x_pair)))
                own = self_f * dt_f[:, h : h + 1] + self_b * dt_b[:, h : h + 1] + skip[h]
                result = part if result is None else result + part
                own = jnp.broadcast_to(own, (rows, PAIR))
                direct = own if direct is None else jnp.where(mine, own, direct)
            head_out[:, columns] = result + direct * x_pair.astype(F32)

    pairs = width // PAIR
    own_part(0, pairs // 2)

    def chain_copy(c):
        return remote(
            chain_out.at[c],
            chain_in.at[c],
            chain_send_sem.at[c],
            chain_recv_sem.at[c],
            seq=following,
        )

    def leaf_copy(c):
        return remote(
            chain_in.at[c],
            leaf_in.at[c],
            leaf_send_sem.at[c],
            leaf_recv_sem.at[c],
            seq=partner,
        )

    def pair_copy(c):
        return remote(
            state_send.at[side, c],
            pair_in.at[c],
            pair_send_sem.at[c],
            pair_recv_sem.at[c],
            seq=partner,
        )

    @pl.when(along == 0)
    def _():
        chain_in[...] = jnp.zeros_like(chain_in)

    @pl.when(leaf_along == 0)
    def _():
        leaf_in[...] = jnp.zeros_like(leaf_in)

    for c in range(chunks):
        pair_copy(c).wait_recv()
        pair_state = pair_in[c, :state].astype(F32)
        pair_tail = pair_in[c, state:].astype(F32)
        pair_decay = pair_tail[0:1] + pair_tail[1:2]
        my_decay = own_decay[node_dir, c][0:1]

        @pl.when(along > 0)
        def _():
            chain_copy(c).wait_recv()
            leaf_copy(c).start()

        entering = pair_decay * chain_in[c].astype(F32) + pair_state
        incoming[node_dir, c] = entering.astype(BF16)

        @pl.when(along < places - 1)
        def _():
            chain_out[c] = (my_decay * entering + own_state[node_dir, c]).astype(BF16)
            chain_copy(c).start()

    own_part(pairs // 2, pairs)
    for load in loads[4:]:
        load.wait()
    for c in range(chunks):
        columns = slice(c * CHUNK, (c + 1) * CHUNK)
        for d in range(2):
            factor[d, :, columns] = widen(grows[d], c)
        gate = gate_ref[0, :, columns].astype(F32)
        silu[:, columns] = gate / (1.0 + jnp.exp(-gate))

    forwards = []
    for i, step in enumerate(range(2, n_dp, 2)):
        w_copies[i].wait_recv()
        owner = lax.rem(my_dp + n_dp - step, n_dp)
        forward = remote(
            w_slot(owner),
            w_slot(owner),
            w_fwd_sem.at[step],
            w_recv_sem.at[step + 1],
            dp=dp_partner,
        )
        forward.start()
        forwards.append(forward)

    for c in range(chunks):
        columns = slice(c * CHUNK, (c + 1) * CHUNK)

        @pl.when(leaf_along > 0)
        def _():
            leaf_copy(c).wait_recv()

        incoming[side, c] = leaf_in[c]
        mixed = (
            head_out[:, columns]
            + dot(c_f, incoming[0, c]) * factor[0, :, columns]
            + dot(c_b, incoming[1, c]) * factor[1, :, columns]
        )
        gated = mixed * silu[:, columns]
        spread_chunk = spread[:, columns]
        square = split(gated * gated)
        mean = (
            dot(square[0], spread_chunk, ((1,), (1,))) + dot(square[1], spread_chunk, ((1,), (1,)))
        ) * (1.0 / head_size)
        scale = widen(split(lax.rsqrt(mean + 1e-05)), c)
        normed[:, columns] = (gated * scale * gain_ref[:, columns]).astype(BF16)

    w_copies[-1].wait_recv()
    for copy in forwards:
        copy.wait_recv()
    for c in range(chunks):
        columns = slice(c * CHUNK, (c + 1) * CHUNK)
        enc_ref[0, :, columns] = dot(normed[...], w_all[:, columns]).astype(BF16)

    encoded = enc_ref[0]
    model = encoded.shape[1]
    queries = latents_ref.shape[0]
    share = queries // n

    def parts_of(values):
        first = values.astype(BF16).astype(F32)
        second = (values - first).astype(BF16).astype(F32)
        third = (values - first - second).astype(BF16).astype(F32)
        return first, second, third

    def tail_of(top, weight):
        at = lax.broadcasted_iota(jnp.int32, (top.shape[0], 128), 1)
        tail = jnp.zeros((top.shape[0], 128), F32)
        for k, part in enumerate(parts_of(top) + parts_of(weight)):
            tail = jnp.where(at == k, part, tail)
        return tail.astype(BF16)

    def read_tail(tail):
        tail = tail.astype(F32)
        top = tail[:, 0:1] + tail[:, 1:2] + tail[:, 2:3]
        return top, tail[:, 3:4] + tail[:, 4:5] + tail[:, 5:6]

    scores = dot(latents_ref[...], encoded, ((1,), (1,))) * (1.0 / math.sqrt(model))
    top = jnp.max(jnp.where(valid, scores, -1e30), axis=1, keepdims=True)
    top = functools.reduce(jnp.add, parts_of(top))
    prob = jnp.where(valid, jnp.exp(scores - top), 0.0)
    weight_sum = jnp.sum(prob, axis=1, keepdims=True)
    tail = tail_of(top, weight_sum).astype(F32).reshape(places, 2, share, 128)
    for s in range(2):
        sum_send[s, :, :, model:] = tail[:, s].astype(BF16)
    prob_low = prob.astype(BF16)
    for c in range(model // CHUNK):
        columns = slice(c * CHUNK, (c + 1) * CHUNK)
        part = dot(prob_low, encoded[:, columns]).reshape(places, 2, share, CHUNK)
        for s in range(2):
            sum_send[s, :, :, columns] = part[:, s].astype(BF16)

    def merge(messages):
        stats = [read_tail(message[:, model:]) for message in messages]
        best = functools.reduce(jnp.maximum, [t for t, _ in stats])
        scales = [jnp.exp(t - best) for t, _ in stats]
        weight = functools.reduce(jnp.add, [w * e for (_, w), e in zip(stats, scales)])
        return best, weight, scales

    def added(messages, scales):
        return functools.reduce(
            jnp.add,
            [message[:, :model].astype(F32) * e for message, e in zip(messages, scales)],
        )

    pair_copies = []
    for step in list(range(1, places)) + [0]:
        target = lax.rem(place + step, places)
        copy = remote(
            sum_send.at[1 - side, target],
            sum_pair.at[step],
            stat_send_sem.at[step],
            stat_recv_sem.at[step],
            seq=partner,
        )
        copy.start()
        pair_copies.append(copy)
    sum_copies = []
    for i, step in enumerate(list(range(1, places)) + [0]):
        target = lax.rem(place + step, places)
        pair_copies[i].wait_recv()
        messages = [sum_send[side, target], sum_pair[step]]
        best, weight, scales = merge(messages)
        sum_both[step, :, :model] = added(messages, scales).astype(BF16)
        sum_both[step, :, model:] = tail_of(best, weight)
        if step > 0:
            copy = remote(
                sum_both.at[step],
                sum_recv.at[step],
                sum_send_sem.at[step],
                sum_recv_sem.at[step],
                seq=2 * target + side,
            )
            copy.start()
            sum_copies.append(copy)
    for copy in sum_copies:
        copy.wait_recv()
    messages = [sum_both[0]] + [sum_recv[step] for step in range(1, places)]
    best, weight, scales = merge(messages)
    inverse = 1.0 / weight
    pool[place, side] = added(messages, [e * inverse for e in scales]).astype(BF16)

    def hand_on(step):
        slot = pool.at[lax.rem(place + places - step, places), side]
        return remote(
            slot, slot, hand_send_sem.at[step], hand_recv_sem.at[step], seq=partner
        )

    pool_copies = []
    for step in range(1, places):
        target = lax.rem(place + step, places)
        copy = remote(
            pool.at[place, side],
            pool.at[place, side],
            pool_send_sem.at[step],
            pool_recv_sem.at[step],
            seq=2 * target + side,
        )
        copy.start()
        pool_copies.append(copy)
    hand_copies = [hand_on(0)]
    hand_copies[0].start()
    for step in range(1, places):
        pool_copies[step - 1].wait_recv()
        copy = hand_on(step)
        copy.start()
        hand_copies.append(copy)
    for copy in hand_copies:
        copy.wait_recv()
    pooled_ref[0] = pool[...].reshape(queries, model)

    for copy in w_copies + forwards + pair_copies + sum_copies + pool_copies + hand_copies:
        copy.wait_send()
    for c in range(chunks):
        pair_copy(c).wait_send()

        @pl.when(along < places - 1)
        def _():
            chain_copy(c).wait_send()

        @pl.when(along > 0)
        def _():
            leaf_copy(c).wait_send()


def body(
    n,
    n_dp,
    ssm_input,
    gate_input,
    state_proj,
    step_raw,
    decay_log,
    skip_gain,
    norm_gain,
    out_weight,
    latents,
    lengths,
):
    rows, width = ssm_input.shape[1], ssm_input.shape[2]
    model = out_weight.shape[1]
    state = state_proj.shape[2] // 4
    queries = latents.shape[0]
    share = queries // n
    chunks = width // CHUNK
    vmem = pl.BlockSpec(memory_space=pltpu.VMEM)
    smem = pl.BlockSpec(memory_space=pltpu.SMEM)
    dma = pltpu.SemaphoreType.DMA
    return pl.pallas_call(
        functools.partial(kernel, n, n_dp),
        out_shape=(
            jax.ShapeDtypeStruct((1, rows, model), BF16),
            jax.ShapeDtypeStruct((1, queries, model), BF16),
        ),
        in_specs=[smem, smem] + [pl.BlockSpec(memory_space=pltpu.HBM)] * 8,
        out_specs=(vmem, vmem),
        scratch_shapes=[
            pltpu.VMEM(ssm_input.shape, BF16),
            pltpu.VMEM(gate_input.shape, BF16),
            pltpu.VMEM(state_proj.shape, BF16),
            pltpu.VMEM(step_raw.shape, F32),
            pltpu.VMEM(decay_log.shape, F32),
            pltpu.VMEM((1, width), F32),
            pltpu.VMEM(latents.shape, BF16),
            pltpu.VMEM((rows, width), F32),
            dma((8,)),
            pltpu.VMEM((width, model), BF16),
            pltpu.VMEM((2, chunks, state, CHUNK), F32),
            pltpu.VMEM((2, chunks, 8, CHUNK), F32),
            pltpu.VMEM((2, chunks, state + 16, CHUNK), BF16),
            pltpu.VMEM((chunks, state + 16, CHUNK), BF16),
            pltpu.VMEM((chunks, state, CHUNK), BF16),
            pltpu.VMEM((chunks, state, CHUNK), BF16),
            pltpu.VMEM((chunks, state, CHUNK), BF16),
            pltpu.VMEM((2, chunks, state, CHUNK), BF16),
            pltpu.VMEM((rows, width), F32),
            pltpu.VMEM((2, rows, width), F32),
            pltpu.VMEM((rows, width), BF16),
            pltpu.VMEM((2, n // 2, share, model + 128), BF16),
            pltpu.VMEM((n // 2, share, model + 128), BF16),
            pltpu.VMEM((n // 2, share, model + 128), BF16),
            pltpu.VMEM((n // 2, share, model + 128), BF16),
            pltpu.VMEM((n // 2, 2, share, model), BF16),
            dma((n_dp,)),
            dma((n_dp,)),
            dma((n_dp,)),
            dma((chunks,)),
            dma((chunks,)),
            dma((chunks,)),
            dma((chunks,)),
            dma((chunks,)),
            dma((chunks,)),
            dma((n // 2,)),
            dma((n // 2,)),
            dma((n // 2,)),
            dma((n // 2,)),
            dma((n // 2,)),
            dma((n // 2,)),
            dma((n // 2,)),
            dma((n // 2,)),
        ],
        compiler_params=pltpu.CompilerParams(
            collective_id=0, has_side_effects=True, vmem_limit_bytes=48 * 1024 * 1024
        ),
    )(
        lengths,
        skip_gain,
        ssm_input,
        gate_input,
        state_proj,
        step_raw,
        decay_log,
        norm_gain.reshape(1, width),
        out_weight,
        latents,
    )


def solution(mesh):
    in_specs = (
        P("dp", "seq", None),
        P("dp", "seq", None),
        P("dp", "seq", None),
        P("dp", None, "seq"),
        P(),
        P(),
        P(),
        P("dp", None),
        P(),
        P("dp"),
    )
    out_specs = (P("dp", "seq", None), P("dp", None, None))
    return jax.shard_map(
        functools.partial(body, mesh.shape["seq"], mesh.shape["dp"]),
        mesh=mesh,
        in_specs=in_specs,
        out_specs=out_specs,
        check_vma=False,
    )
```

```python
import functools
import math

import jax
import jax.numpy as jnp
from jax import lax
from jax.experimental import pallas as pl
from jax.experimental.pallas import tpu as pltpu
from jax.sharding import PartitionSpec as P

CHUNK = 256
PAIR = 128
VMEM_BYTES = 63 * 1024 * 1024 + 512 * 1024
F32 = jnp.float32
BF16 = jnp.bfloat16


def dot(a, b, dims=((1,), (0,)), precision=None):
    return lax.dot_general(
        a, b, (dims, ((), ())), precision=precision, preferred_element_type=F32
    )


def column_of(row, size):
    eye = lax.broadcasted_iota(jnp.int32, (size, size), 0) == lax.broadcasted_iota(
        jnp.int32, (size, size), 1
    )
    return jnp.sum(jnp.where(eye, jnp.broadcast_to(row, (size, size)), 0.0), axis=1, keepdims=True)


def kernel(
    n,
    n_dp,
    lengths,
    skip,
    x_hbm,
    gate_hbm,
    proj_hbm,
    raw_hbm,
    decay_hbm,
    gain_hbm,
    w_ref,
    latents_hbm,
    enc_ref,
    pooled_ref,
    x_ref,
    gate_ref,
    proj_ref,
    raw_ref,
    decay_ref,
    gain_ref,
    latents_ref,
    silu,
    load_sem,
    w_all,
    own_state,
    own_decay,
    state_send,
    pair_in,
    chain_in,
    chain_out,
    leaf_in,
    incoming,
    head_out,
    factor,
    normed,
    sum_send,
    sum_pair,
    sum_both,
    sum_recv,
    pool,
    w_send_sem,
    w_fwd_sem,
    w_recv_sem,
    pair_send_sem,
    pair_recv_sem,
    chain_send_sem,
    chain_recv_sem,
    leaf_send_sem,
    leaf_recv_sem,
    sum_send_sem,
    sum_recv_sem,
    stat_send_sem,
    stat_recv_sem,
    pool_send_sem,
    pool_recv_sem,
    hand_send_sem,
    hand_recv_sem,
):
    rows, width = x_ref.shape[1], x_ref.shape[2]
    heads = decay_ref.shape[1]
    head_size = width // heads
    state = proj_ref.shape[2] // 4
    chunks = width // CHUNK
    w_rows = w_ref.shape[0]
    me = lax.axis_index("seq")
    my_dp = lax.axis_index("dp")

    def remote(src, dst, send_sem, recv_sem, seq=None, dp=None):
        device_id = {"seq": seq} if dp is None else {"dp": dp}
        return pltpu.make_async_remote_copy(
            src_ref=src,
            dst_ref=dst,
            send_sem=send_sem,
            recv_sem=recv_sem,
            device_id=device_id,
            device_id_type=pl.DeviceIdType.MESH,
        )

    side = lax.rem(me, 2)
    place = me // 2
    places = n // 2
    partner = me + 1 - 2 * side
    node_dir = 1 - side
    along = jnp.where(side == 1, place, places - 1 - place)
    leaf_along = jnp.where(side == 1, places - 1 - place, place)
    following = lax.rem(me + 4 * side - 2 + n, n)
    core = lax.rem(my_dp, 2)
    dp_partner = my_dp + 1 - 2 * core

    loads = [
        pltpu.make_async_copy(source, target, load_sem.at[i])
        for i, (source, target) in enumerate(
            (
                (raw_hbm, raw_ref),
                (decay_hbm, decay_ref),
                (proj_hbm, proj_ref),
                (x_hbm, x_ref),
                (gate_hbm, gate_ref),
                (gain_hbm, gain_ref),
                (latents_hbm, latents_ref),
                (w_ref, w_all.at[pl.ds(pl.multiple_of(my_dp * w_rows, w_rows), w_rows)]),
            )
        )
    ]
    for load in loads:
        load.start()

    barrier = pltpu.get_barrier_semaphore()
    for neighbour in [partner] + [
        2 * lax.rem(place + step, places) + side for step in range(1, places)
    ]:
        pl.semaphore_signal(
            barrier,
            inc=1,
            device_id={"seq": neighbour},
            device_id_type=pl.DeviceIdType.MESH,
        )
    pl.semaphore_signal(
        barrier, inc=1, device_id={"dp": dp_partner}, device_id_type=pl.DeviceIdType.MESH
    )
    for step in range(2, n_dp, 2):
        pl.semaphore_signal(
            barrier,
            inc=1,
            device_id={"dp": lax.rem(my_dp + step, n_dp)},
            device_id_type=pl.DeviceIdType.MESH,
        )
    pl.semaphore_wait(barrier, places + n_dp // 2)

    def w_slot(owner):
        return w_all.at[pl.ds(pl.multiple_of(owner * w_rows, w_rows), w_rows)]

    w_copies = []
    for step in range(2, n_dp, 2):
        w_copies.append(
            remote(
                w_ref,
                w_slot(my_dp),
                w_send_sem.at[step],
                w_recv_sem.at[step],
                dp=lax.rem(my_dp + step, n_dp),
            )
        )
    w_copies.append(
        remote(w_ref, w_slot(my_dp), w_send_sem.at[0], w_recv_sem.at[0], dp=dp_partner)
    )
    for copy in w_copies:
        copy.start()

    for load in loads[:4]:
        load.wait()

    token = lax.broadcasted_iota(jnp.int32, (1, rows), 1)
    valid = (me * rows + token) < lengths[0]
    raw = raw_ref[0]
    softplus = jnp.maximum(raw, 0.0) + jnp.log1p(jnp.exp(-jnp.abs(raw)))
    dt = jnp.where(valid, softplus, 0.0)
    rates = jnp.exp(decay_ref[...])
    step_f, step_b = dt[:heads], dt[heads:]
    loss_f = -step_f * column_of(rates[0:1], heads)
    loss_b = -step_b * column_of(rates[1:2], heads)
    row_at = lax.broadcasted_iota(jnp.int32, (rows, rows), 0)
    col_at = lax.broadcasted_iota(jnp.int32, (rows, rows), 1)
    cum_f = dot(loss_f, jnp.where(row_at <= col_at, 1.0, 0.0), precision=lax.Precision.HIGHEST)
    cum_b = dot(loss_b, jnp.where(row_at >= col_at, 1.0, 0.0), precision=lax.Precision.HIGHEST)
    stacked = jnp.concatenate(
        [cum_f, cum_b, step_f, step_b, jnp.zeros((128 - 4 * heads, rows), F32)], axis=0
    )
    by_token = stacked.T
    col_f, col_b = by_token[:, :heads], by_token[:, heads : 2 * heads]
    dt_f, dt_b = by_token[:, 2 * heads : 3 * heads], by_token[:, 3 * heads : 4 * heads]
    tail_f = jnp.exp(col_f[rows - 1 : rows] - col_f) * dt_f
    tail_b = jnp.exp(col_b[0:1] - col_b) * dt_b
    grow_f, grow_b = jnp.exp(col_f), jnp.exp(col_b)

    head_row = lax.broadcasted_iota(jnp.int32, (heads, width), 0) * head_size
    head_lane = lax.broadcasted_iota(jnp.int32, (heads, width), 1)
    spread = jnp.where(
        (head_lane >= head_row) & (head_lane < head_row + head_size), 1.0, 0.0
    ).astype(BF16)

    def split(values):
        high = values.astype(BF16)
        return high, (values - high.astype(F32)).astype(BF16)

    def widen(parts, c):
        columns = spread[:, c * CHUNK : (c + 1) * CHUNK]
        return dot(parts[0], columns) + dot(parts[1], columns)

    proj = proj_ref[0]
    b_f, c_f = proj[:, :state], proj[:, state : 2 * state]
    b_b, c_b = proj[:, 2 * state : 3 * state], proj[:, 3 * state :]

    tails = (split(tail_f), split(tail_b))
    grows = (split(grow_f), split(grow_b))
    ends = (
        split(jnp.broadcast_to(grow_f[rows - 1 : rows], (8, heads))),
        split(jnp.broadcast_to(grow_b[0:1], (8, heads))),
    )
    tail_row = lax.broadcasted_iota(jnp.int32, (16, CHUNK), 0)
    for c in range(chunks):
        columns = slice(c * CHUNK, (c + 1) * CHUNK)
        x_chunk = x_ref[0, :, columns].astype(F32)
        for d, b_d in ((0, b_f), (1, b_b)):
            scaled = (x_chunk * widen(tails[d], c)).astype(BF16)
            total = dot(b_d, scaled, ((0,), (0,)))
            decay = widen(ends[d], c)
            own_state[d, c] = total
            own_decay[d, c] = decay
            state_send[d, c, :state] = total.astype(BF16)
            high, low = split(decay[0:1])
            state_send[d, c, state:] = jnp.where(
                tail_row == 0,
                high.astype(F32),
                jnp.where(tail_row == 1, low.astype(F32), 0.0),
            ).astype(BF16)
        remote(
            state_send.at[side, c],
            pair_in.at[c],
            pair_send_sem.at[c],
            pair_recv_sem.at[c],
            seq=partner,
        ).start()

    gram_f = dot(c_f, b_f, ((1,), (1,)))
    gram_b = dot(c_b, b_b, ((1,), (1,)))
    earlier = col_at < row_at
    gram = jnp.where(earlier, gram_f, jnp.where(col_at == row_at, 0.0, gram_b))
    self_f = jnp.sum(c_f.astype(F32) * b_f.astype(F32), axis=1, keepdims=True)
    self_b = jnp.sum(c_b.astype(F32) * b_b.astype(F32), axis=1, keepdims=True)
    lane = lax.broadcasted_iota(jnp.int32, (rows, PAIR), 1)

    def own_part(first_pair, last_pair):
        for pair in range(first_pair, last_pair):
            columns = slice(pair * PAIR, (pair + 1) * PAIR)
            x_pair = x_ref[0, :, columns]
            result = None
            direct = None
            for k in range(PAIR // head_size):
                h = pair * (PAIR // head_size) + k
                gap = jnp.where(
                    earlier,
                    col_f[:, h : h + 1] - cum_f[h : h + 1],
                    col_b[:, h : h + 1] - cum_b[h : h + 1],
                )
                weight = jnp.where(earlier, step_f[h : h + 1], step_b[h : h + 1])
                mixing = (gram * jnp.exp(gap) * weight).astype(BF16)
                mine = (lane >= k * head_size) & (lane < (k + 1) * head_size)
                part = dot(mixing, jnp.where(mine, x_pair, jnp.zeros_like(x_pair)))
                own = self_f * dt_f[:, h : h + 1] + self_b * dt_b[:, h : h + 1] + skip[h]
                result = part if result is None else result + part
                own = jnp.broadcast_to(own, (rows, PAIR))
                direct = own if direct is None else jnp.where(mine, own, direct)
            head_out[:, columns] = result + direct * x_pair.astype(F32)

    pairs = width // PAIR
    pl.when(along >= 1)(lambda: own_part(0, pairs // 2))
    pl.when(along >= 2)(lambda: own_part(pairs // 2, pairs))

    def chain_copy(c):
        return remote(
            chain_out.at[c],
            chain_in.at[c],
            chain_send_sem.at[c],
            chain_recv_sem.at[c],
            seq=following,
        )

    def leaf_copy(c):
        return remote(
            chain_in.at[c],
            leaf_in.at[c],
            leaf_send_sem.at[c],
            leaf_recv_sem.at[c],
            seq=partner,
        )

    def pair_copy(c):
        return remote(
            state_send.at[side, c],
            pair_in.at[c],
            pair_send_sem.at[c],
            pair_recv_sem.at[c],
            seq=partner,
        )

    @pl.when(along == 0)
    def _():
        chain_in[...] = jnp.zeros_like(chain_in)

    @pl.when(leaf_along == 0)
    def _():
        leaf_in[...] = jnp.zeros_like(leaf_in)

    for c in range(chunks):
        pair_copy(c).wait_recv()
        pair_state = pair_in[c, :state].astype(F32)
        pair_tail = pair_in[c, state:].astype(F32)
        pair_decay = pair_tail[0:1] + pair_tail[1:2]
        my_decay = own_decay[node_dir, c][0:1]

        @pl.when(along > 0)
        def _():
            chain_copy(c).wait_recv()
            leaf_copy(c).start()

        entering = pair_decay * chain_in[c].astype(F32) + pair_state
        incoming[node_dir, c] = entering.astype(BF16)

        @pl.when(along < places - 1)
        def _():
            chain_out[c] = (my_decay * entering + own_state[node_dir, c]).astype(BF16)
            chain_copy(c).start()

    pl.when(along < 1)(lambda: own_part(0, pairs // 2))
    pl.when(along < 2)(lambda: own_part(pairs // 2, pairs))
    for load in loads[4:]:
        load.wait()
    for c in range(chunks):
        columns = slice(c * CHUNK, (c + 1) * CHUNK)
        for d in range(2):
            factor[d, :, columns] = widen(grows[d], c)
        gate = gate_ref[0, :, columns].astype(F32)
        silu[:, columns] = gate / (1.0 + jnp.exp(-gate))

    forwards = []
    for i, step in enumerate(range(2, n_dp, 2)):
        w_copies[i].wait_recv()
        owner = lax.rem(my_dp + n_dp - step, n_dp)
        forward = remote(
            w_slot(owner),
            w_slot(owner),
            w_fwd_sem.at[step],
            w_recv_sem.at[step + 1],
            dp=dp_partner,
        )
        forward.start()
        forwards.append(forward)

    for c in range(chunks):
        columns = slice(c * CHUNK, (c + 1) * CHUNK)

        @pl.when(leaf_along > 0)
        def _():
            leaf_copy(c).wait_recv()

        incoming[side, c] = leaf_in[c]
        mixed = (
            head_out[:, columns]
            + dot(c_f, incoming[0, c]) * factor[0, :, columns]
            + dot(c_b, incoming[1, c]) * factor[1, :, columns]
        )
        gated = mixed * silu[:, columns]
        spread_chunk = spread[:, columns]
        square = split(gated * gated)
        mean = (
            dot(square[0], spread_chunk, ((1,), (1,))) + dot(square[1], spread_chunk, ((1,), (1,)))
        ) * (1.0 / head_size)
        scale = widen(split(lax.rsqrt(mean + 1e-05)), c)
        normed[:, columns] = (gated * scale * gain_ref[:, columns]).astype(BF16)

    w_copies[-1].wait_recv()
    for copy in forwards:
        copy.wait_recv()
    for c in range(chunks):
        columns = slice(c * CHUNK, (c + 1) * CHUNK)
        enc_ref[0, :, columns] = dot(normed[...], w_all[:, columns]).astype(BF16)

    encoded = enc_ref[0]
    model = encoded.shape[1]
    queries = latents_ref.shape[0]
    share = queries // n

    def parts_of(values):
        first = values.astype(BF16).astype(F32)
        second = (values - first).astype(BF16).astype(F32)
        third = (values - first - second).astype(BF16).astype(F32)
        return first, second, third

    def tail_of(top, weight):
        at = lax.broadcasted_iota(jnp.int32, (top.shape[0], 128), 1)
        tail = jnp.zeros((top.shape[0], 128), F32)
        for k, part in enumerate(parts_of(top) + parts_of(weight)):
            tail = jnp.where(at == k, part, tail)
        return tail.astype(BF16)

    def read_tail(tail):
        tail = tail.astype(F32)
        top = tail[:, 0:1] + tail[:, 1:2] + tail[:, 2:3]
        return top, tail[:, 3:4] + tail[:, 4:5] + tail[:, 5:6]

    scores = dot(latents_ref[...], encoded, ((1,), (1,))) * (1.0 / math.sqrt(model))
    top = jnp.max(jnp.where(valid, scores, -1e30), axis=1, keepdims=True)
    top = functools.reduce(jnp.add, parts_of(top))
    prob = jnp.where(valid, jnp.exp(scores - top), 0.0)
    weight_sum = jnp.sum(prob, axis=1, keepdims=True)
    tail = tail_of(top, weight_sum).astype(F32).reshape(places, 2, share, 128)
    for s in range(2):
        sum_send[s, :, :, model:] = tail[:, s].astype(BF16)
    prob_low = prob.astype(BF16)
    for c in range(model // CHUNK):
        columns = slice(c * CHUNK, (c + 1) * CHUNK)
        part = dot(prob_low, encoded[:, columns]).reshape(places, 2, share, CHUNK)
        for s in range(2):
            sum_send[s, :, :, columns] = part[:, s].astype(BF16)

    def merge(messages):
        stats = [read_tail(message[:, model:]) for message in messages]
        best = functools.reduce(jnp.maximum, [t for t, _ in stats])
        scales = [jnp.exp(t - best) for t, _ in stats]
        weight = functools.reduce(jnp.add, [w * e for (_, w), e in zip(stats, scales)])
        return best, weight, scales

    def added(messages, scales):
        return functools.reduce(
            jnp.add,
            [message[:, :model].astype(F32) * e for message, e in zip(messages, scales)],
        )

    pair_copies = []
    for step in list(range(1, places)) + [0]:
        target = lax.rem(place + step, places)
        copy = remote(
            sum_send.at[1 - side, target],
            sum_pair.at[step],
            stat_send_sem.at[step],
            stat_recv_sem.at[step],
            seq=partner,
        )
        copy.start()
        pair_copies.append(copy)
    sum_copies = []
    for i, step in enumerate(list(range(1, places)) + [0]):
        target = lax.rem(place + step, places)
        pair_copies[i].wait_recv()
        messages = [sum_send[side, target], sum_pair[step]]
        best, weight, scales = merge(messages)
        sum_both[step, :, :model] = added(messages, scales).astype(BF16)
        sum_both[step, :, model:] = tail_of(best, weight)
        if step > 0:
            copy = remote(
                sum_both.at[step],
                sum_recv.at[step],
                sum_send_sem.at[step],
                sum_recv_sem.at[step],
                seq=2 * target + side,
            )
            copy.start()
            sum_copies.append(copy)
    for copy in sum_copies:
        copy.wait_recv()
    messages = [sum_both[0]] + [sum_recv[step] for step in range(1, places)]
    best, weight, scales = merge(messages)
    inverse = 1.0 / weight
    pool[place, side] = added(messages, [e * inverse for e in scales]).astype(BF16)

    def hand_on(step):
        slot = pool.at[lax.rem(place + places - step, places), side]
        return remote(
            slot, slot, hand_send_sem.at[step], hand_recv_sem.at[step], seq=partner
        )

    pool_copies = []
    for step in range(1, places):
        target = lax.rem(place + step, places)
        copy = remote(
            pool.at[place, side],
            pool.at[place, side],
            pool_send_sem.at[step],
            pool_recv_sem.at[step],
            seq=2 * target + side,
        )
        copy.start()
        pool_copies.append(copy)
    hand_copies = [hand_on(0)]
    hand_copies[0].start()
    for step in range(1, places):
        pool_copies[step - 1].wait_recv()
        copy = hand_on(step)
        copy.start()
        hand_copies.append(copy)
    for copy in hand_copies:
        copy.wait_recv()
    pooled_ref[0] = pool[...].reshape(queries, model)

    for copy in w_copies + forwards + pair_copies + sum_copies + pool_copies + hand_copies:
        copy.wait_send()
    for c in range(chunks):
        pair_copy(c).wait_send()

        @pl.when(along < places - 1)
        def _():
            chain_copy(c).wait_send()

        @pl.when(along > 0)
        def _():
            leaf_copy(c).wait_send()


def body(
    n,
    n_dp,
    ssm_input,
    gate_input,
    state_proj,
    step_raw,
    decay_log,
    skip_gain,
    norm_gain,
    out_weight,
    latents,
    lengths,
):
    rows, width = ssm_input.shape[1], ssm_input.shape[2]
    model = out_weight.shape[1]
    state = state_proj.shape[2] // 4
    queries = latents.shape[0]
    share = queries // n
    chunks = width // CHUNK
    vmem = pl.BlockSpec(memory_space=pltpu.VMEM)
    smem = pl.BlockSpec(memory_space=pltpu.SMEM)
    dma = pltpu.SemaphoreType.DMA
    return pl.pallas_call(
        functools.partial(kernel, n, n_dp),
        out_shape=(
            jax.ShapeDtypeStruct((1, rows, model), BF16),
            jax.ShapeDtypeStruct((1, queries, model), BF16),
        ),
        in_specs=[smem, smem] + [pl.BlockSpec(memory_space=pltpu.HBM)] * 8,
        out_specs=(vmem, vmem),
        scratch_shapes=[
            pltpu.VMEM(ssm_input.shape, BF16),
            pltpu.VMEM(gate_input.shape, BF16),
            pltpu.VMEM(state_proj.shape, BF16),
            pltpu.VMEM(step_raw.shape, F32),
            pltpu.VMEM(decay_log.shape, F32),
            pltpu.VMEM((1, width), F32),
            pltpu.VMEM(latents.shape, BF16),
            pltpu.VMEM((rows, width), F32),
            dma((8,)),
            pltpu.VMEM((width, model), BF16),
            pltpu.VMEM((2, chunks, state, CHUNK), F32),
            pltpu.VMEM((2, chunks, 8, CHUNK), F32),
            pltpu.VMEM((2, chunks, state + 16, CHUNK), BF16),
            pltpu.VMEM((chunks, state + 16, CHUNK), BF16),
            pltpu.VMEM((chunks, state, CHUNK), BF16),
            pltpu.VMEM((chunks, state, CHUNK), BF16),
            pltpu.VMEM((chunks, state, CHUNK), BF16),
            pltpu.VMEM((2, chunks, state, CHUNK), BF16),
            pltpu.VMEM((rows, width), F32),
            pltpu.VMEM((2, rows, width), F32),
            pltpu.VMEM((rows, width), BF16),
            pltpu.VMEM((2, n // 2, share, model + 128), BF16),
            pltpu.VMEM((n // 2, share, model + 128), BF16),
            pltpu.VMEM((n // 2, share, model + 128), BF16),
            pltpu.VMEM((n // 2, share, model + 128), BF16),
            pltpu.VMEM((n // 2, 2, share, model), BF16),
            dma((n_dp,)),
            dma((n_dp,)),
            dma((n_dp,)),
            dma((chunks,)),
            dma((chunks,)),
            dma((chunks,)),
            dma((chunks,)),
            dma((chunks,)),
            dma((chunks,)),
            dma((n // 2,)),
            dma((n // 2,)),
            dma((n // 2,)),
            dma((n // 2,)),
            dma((n // 2,)),
            dma((n // 2,)),
            dma((n // 2,)),
            dma((n // 2,)),
        ],
        compiler_params=pltpu.CompilerParams(
            collective_id=0, has_side_effects=True, vmem_limit_bytes=VMEM_BYTES
        ),
    )(
        lengths,
        skip_gain,
        ssm_input,
        gate_input,
        state_proj,
        step_raw,
        decay_log,
        norm_gain.reshape(1, width),
        out_weight,
        latents,
    )


def solution(mesh):
    in_specs = (
        P("dp", "seq", None),
        P("dp", "seq", None),
        P("dp", "seq", None),
        P("dp", None, "seq"),
        P(),
        P(),
        P(),
        P("dp", None),
        P(),
        P("dp"),
    )
    out_specs = (P("dp", "seq", None), P("dp", None, None))
    return jax.shard_map(
        functools.partial(body, mesh.shape["seq"], mesh.shape["dp"]),
        mesh=mesh,
        in_specs=in_specs,
        out_specs=out_specs,
        check_vma=False,
    )
```

```python
import functools
import math

import jax
import jax.numpy as jnp
from jax import lax
from jax.experimental import pallas as pl
from jax.experimental.pallas import tpu as pltpu
from jax.sharding import PartitionSpec as P

CHUNK = 256
PAIR = 128
VMEM_BYTES = 63 * 1024 * 1024 + 512 * 1024
F32 = jnp.float32
BF16 = jnp.bfloat16


def dot(a, b, dims=((1,), (0,)), precision=None):
    return lax.dot_general(
        a, b, (dims, ((), ())), precision=precision, preferred_element_type=F32
    )


def column_of(row, size):
    eye = lax.broadcasted_iota(jnp.int32, (size, size), 0) == lax.broadcasted_iota(
        jnp.int32, (size, size), 1
    )
    return jnp.sum(jnp.where(eye, jnp.broadcast_to(row, (size, size)), 0.0), axis=1, keepdims=True)


def kernel(
    n,
    n_dp,
    lengths,
    skip,
    x_hbm,
    gate_hbm,
    proj_hbm,
    raw_hbm,
    decay_hbm,
    gain_hbm,
    w_ref,
    latents_hbm,
    enc_ref,
    pooled_ref,
    x_ref,
    gate_ref,
    proj_ref,
    raw_ref,
    decay_ref,
    gain_ref,
    latents_ref,
    silu,
    load_sem,
    w_all,
    own_state,
    own_decay,
    state_send,
    pair_in,
    chain_in,
    chain_out,
    leaf_in,
    incoming,
    head_out,
    factor,
    normed,
    sum_send,
    sum_pair,
    sum_both,
    sum_recv,
    pool,
    w_send_sem,
    w_fwd_sem,
    w_recv_sem,
    pair_send_sem,
    pair_recv_sem,
    chain_send_sem,
    chain_recv_sem,
    leaf_send_sem,
    leaf_recv_sem,
    sum_send_sem,
    sum_recv_sem,
    stat_send_sem,
    stat_recv_sem,
    pool_send_sem,
    pool_recv_sem,
    hand_send_sem,
    hand_recv_sem,
):
    rows, width = x_ref.shape[1], x_ref.shape[2]
    heads = decay_ref.shape[1]
    head_size = width // heads
    state = proj_ref.shape[2] // 4
    chunks = width // CHUNK
    w_rows = w_ref.shape[0]
    me = lax.axis_index("seq")
    my_dp = lax.axis_index("dp")

    def remote(src, dst, send_sem, recv_sem, seq=None, dp=None):
        device_id = {"seq": seq} if dp is None else {"dp": dp}
        return pltpu.make_async_remote_copy(
            src_ref=src,
            dst_ref=dst,
            send_sem=send_sem,
            recv_sem=recv_sem,
            device_id=device_id,
            device_id_type=pl.DeviceIdType.MESH,
        )

    side = lax.rem(me, 2)
    place = me // 2
    places = n // 2
    partner = me + 1 - 2 * side
    node_dir = 1 - side
    along = jnp.where(side == 1, place, places - 1 - place)
    leaf_along = jnp.where(side == 1, places - 1 - place, place)
    following = lax.rem(me + 4 * side - 2 + n, n)
    core = lax.rem(my_dp, 2)
    dp_partner = my_dp + 1 - 2 * core

    loads = [
        pltpu.make_async_copy(source, target, load_sem.at[i])
        for i, (source, target) in enumerate(
            (
                (raw_hbm, raw_ref),
                (decay_hbm, decay_ref),
                (proj_hbm, proj_ref),
                (x_hbm, x_ref),
                (gate_hbm, gate_ref),
                (gain_hbm, gain_ref),
                (latents_hbm, latents_ref),
                (w_ref, w_all.at[pl.ds(pl.multiple_of(my_dp * w_rows, w_rows), w_rows)]),
            )
        )
    ]
    for load in loads:
        load.start()

    barrier = pltpu.get_barrier_semaphore()
    for neighbour in [partner] + [
        2 * lax.rem(place + step, places) + side for step in range(1, places)
    ]:
        pl.semaphore_signal(
            barrier,
            inc=1,
            device_id={"seq": neighbour},
            device_id_type=pl.DeviceIdType.MESH,
        )
    pl.semaphore_signal(
        barrier, inc=1, device_id={"dp": dp_partner}, device_id_type=pl.DeviceIdType.MESH
    )
    for step in range(2, n_dp, 2):
        pl.semaphore_signal(
            barrier,
            inc=1,
            device_id={"dp": lax.rem(my_dp + step, n_dp)},
            device_id_type=pl.DeviceIdType.MESH,
        )
    pl.semaphore_wait(barrier, places + n_dp // 2)

    def w_slot(owner):
        return w_all.at[pl.ds(pl.multiple_of(owner * w_rows, w_rows), w_rows)]

    w_copies = []
    for step in range(2, n_dp, 2):
        w_copies.append(
            remote(
                w_ref,
                w_slot(my_dp),
                w_send_sem.at[step],
                w_recv_sem.at[step],
                dp=lax.rem(my_dp + step, n_dp),
            )
        )
    w_copies.append(
        remote(w_ref, w_slot(my_dp), w_send_sem.at[0], w_recv_sem.at[0], dp=dp_partner)
    )
    for copy in w_copies:
        copy.start()

    for load in loads[:4]:
        load.wait()

    token = lax.broadcasted_iota(jnp.int32, (1, rows), 1)
    valid = (me * rows + token) < lengths[0]
    raw = raw_ref[0]
    softplus = jnp.maximum(raw, 0.0) + jnp.log1p(jnp.exp(-jnp.abs(raw)))
    dt = jnp.where(valid, softplus, 0.0)
    rates = jnp.exp(decay_ref[...])
    step_f, step_b = dt[:heads], dt[heads:]
    loss_f = -step_f * column_of(rates[0:1], heads)
    loss_b = -step_b * column_of(rates[1:2], heads)
    row_at = lax.broadcasted_iota(jnp.int32, (rows, rows), 0)
    col_at = lax.broadcasted_iota(jnp.int32, (rows, rows), 1)
    cum_f = dot(loss_f, jnp.where(row_at <= col_at, 1.0, 0.0), precision=lax.Precision.HIGHEST)
    cum_b = dot(loss_b, jnp.where(row_at >= col_at, 1.0, 0.0), precision=lax.Precision.HIGHEST)
    stacked = jnp.concatenate(
        [cum_f, cum_b, step_f, step_b, jnp.zeros((128 - 4 * heads, rows), F32)], axis=0
    )
    by_token = stacked.T
    col_f, col_b = by_token[:, :heads], by_token[:, heads : 2 * heads]
    dt_f, dt_b = by_token[:, 2 * heads : 3 * heads], by_token[:, 3 * heads : 4 * heads]
    tail_f = jnp.exp(col_f[rows - 1 : rows] - col_f) * dt_f
    tail_b = jnp.exp(col_b[0:1] - col_b) * dt_b
    grow_f, grow_b = jnp.exp(col_f), jnp.exp(col_b)

    head_row = lax.broadcasted_iota(jnp.int32, (heads, width), 0) * head_size
    head_lane = lax.broadcasted_iota(jnp.int32, (heads, width), 1)
    spread = jnp.where(
        (head_lane >= head_row) & (head_lane < head_row + head_size), 1.0, 0.0
    ).astype(BF16)

    def split(values):
        high = values.astype(BF16)
        return high, (values - high.astype(F32)).astype(BF16)

    def widen(parts, c):
        columns = spread[:, c * CHUNK : (c + 1) * CHUNK]
        return dot(parts[0], columns) + dot(parts[1], columns)

    proj = proj_ref[0]
    b_f, c_f = proj[:, :state], proj[:, state : 2 * state]
    b_b, c_b = proj[:, 2 * state : 3 * state], proj[:, 3 * state :]

    tails = (split(tail_f), split(tail_b))
    grows = (split(grow_f), split(grow_b))
    ends = (
        split(jnp.broadcast_to(grow_f[rows - 1 : rows], (8, heads))),
        split(jnp.broadcast_to(grow_b[0:1], (8, heads))),
    )
    tail_row = lax.broadcasted_iota(jnp.int32, (16, CHUNK), 0)
    for c in range(chunks):
        columns = slice(c * CHUNK, (c + 1) * CHUNK)
        x_chunk = x_ref[0, :, columns].astype(F32)
        for d, b_d in ((0, b_f), (1, b_b)):
            scaled = (x_chunk * widen(tails[d], c)).astype(BF16)
            total = dot(b_d, scaled, ((0,), (0,)))
            decay = widen(ends[d], c)
            own_state[d, c] = total
            own_decay[d, c] = decay
            state_send[d, c, :state] = total.astype(BF16)
            high, low = split(decay[0:1])
            state_send[d, c, state:] = jnp.where(
                tail_row == 0,
                high.astype(F32),
                jnp.where(tail_row == 1, low.astype(F32), 0.0),
            ).astype(BF16)
        remote(
            state_send.at[side, c],
            pair_in.at[c],
            pair_send_sem.at[c],
            pair_recv_sem.at[c],
            seq=partner,
        ).start()

    gram_f = dot(c_f, b_f, ((1,), (1,)))
    gram_b = dot(c_b, b_b, ((1,), (1,)))
    earlier = col_at < row_at
    gram = jnp.where(earlier, gram_f, jnp.where(col_at == row_at, 0.0, gram_b))
    self_f = jnp.sum(c_f.astype(F32) * b_f.astype(F32), axis=1, keepdims=True)
    self_b = jnp.sum(c_b.astype(F32) * b_b.astype(F32), axis=1, keepdims=True)
    lane = lax.broadcasted_iota(jnp.int32, (rows, PAIR), 1)

    def own_part(first_pair, last_pair):
        for pair in range(first_pair, last_pair):
            columns = slice(pair * PAIR, (pair + 1) * PAIR)
            x_pair = x_ref[0, :, columns]
            result = None
            direct = None
            for k in range(PAIR // head_size):
                h = pair * (PAIR // head_size) + k
                gap = jnp.where(
                    earlier,
                    col_f[:, h : h + 1] - cum_f[h : h + 1],
                    col_b[:, h : h + 1] - cum_b[h : h + 1],
                )
                weight = jnp.where(earlier, step_f[h : h + 1], step_b[h : h + 1])
                mixing = (gram * jnp.exp(gap) * weight).astype(BF16)
                mine = (lane >= k * head_size) & (lane < (k + 1) * head_size)
                part = dot(mixing, jnp.where(mine, x_pair, jnp.zeros_like(x_pair)))
                own = self_f * dt_f[:, h : h + 1] + self_b * dt_b[:, h : h + 1] + skip[h]
                result = part if result is None else result + part
                own = jnp.broadcast_to(own, (rows, PAIR))
                direct = own if direct is None else jnp.where(mine, own, direct)
            head_out[:, columns] = result + direct * x_pair.astype(F32)

    def prepare():
        for load in loads[4:7]:
            load.wait()
        for c in range(chunks):
            columns = slice(c * CHUNK, (c + 1) * CHUNK)
            for d in range(2):
                factor[d, :, columns] = widen(grows[d], c)
            gate = gate_ref[0, :, columns].astype(F32)
            silu[:, columns] = gate / (1.0 + jnp.exp(-gate))

    pairs = width // PAIR
    pl.when(along >= 1)(lambda: own_part(0, pairs // 2))
    pl.when(along >= 2)(lambda: own_part(pairs // 2, pairs))
    pl.when(along >= 2)(prepare)

    def chain_copy(c):
        return remote(
            chain_out.at[c],
            chain_in.at[c],
            chain_send_sem.at[c],
            chain_recv_sem.at[c],
            seq=following,
        )

    def leaf_copy(c):
        return remote(
            chain_in.at[c],
            leaf_in.at[c],
            leaf_send_sem.at[c],
            leaf_recv_sem.at[c],
            seq=partner,
        )

    def pair_copy(c):
        return remote(
            state_send.at[side, c],
            pair_in.at[c],
            pair_send_sem.at[c],
            pair_recv_sem.at[c],
            seq=partner,
        )

    @pl.when(along == 0)
    def _():
        chain_in[...] = jnp.zeros_like(chain_in)

    @pl.when(leaf_along == 0)
    def _():
        leaf_in[...] = jnp.zeros_like(leaf_in)

    for c in range(chunks):
        pair_copy(c).wait_recv()
        pair_state = pair_in[c, :state].astype(F32)
        pair_tail = pair_in[c, state:].astype(F32)
        pair_decay = pair_tail[0:1] + pair_tail[1:2]
        my_decay = own_decay[node_dir, c][0:1]

        @pl.when(along > 0)
        def _():
            chain_copy(c).wait_recv()
            leaf_copy(c).start()

        entering = pair_decay * chain_in[c].astype(F32) + pair_state
        incoming[node_dir, c] = entering.astype(BF16)

        @pl.when(along < places - 1)
        def _():
            chain_out[c] = (my_decay * entering + own_state[node_dir, c]).astype(BF16)
            chain_copy(c).start()

    pl.when(along < 1)(lambda: own_part(0, pairs // 2))
    pl.when(along < 2)(lambda: own_part(pairs // 2, pairs))
    pl.when(along < 2)(prepare)

    loads[7].wait()
    forwards = []
    for i, step in enumerate(range(2, n_dp, 2)):
        w_copies[i].wait_recv()
        owner = lax.rem(my_dp + n_dp - step, n_dp)
        forward = remote(
            w_slot(owner),
            w_slot(owner),
            w_fwd_sem.at[step],
            w_recv_sem.at[step + 1],
            dp=dp_partner,
        )
        forward.start()
        forwards.append(forward)

    for c in range(chunks):
        columns = slice(c * CHUNK, (c + 1) * CHUNK)

        @pl.when(leaf_along > 0)
        def _():
            leaf_copy(c).wait_recv()

        incoming[side, c] = leaf_in[c]
        mixed = (
            head_out[:, columns]
            + dot(c_f, incoming[0, c]) * factor[0, :, columns]
            + dot(c_b, incoming[1, c]) * factor[1, :, columns]
        )
        gated = mixed * silu[:, columns]
        spread_chunk = spread[:, columns]
        square = split(gated * gated)
        mean = (
            dot(square[0], spread_chunk, ((1,), (1,))) + dot(square[1], spread_chunk, ((1,), (1,)))
        ) * (1.0 / head_size)
        scale = widen(split(lax.rsqrt(mean + 1e-05)), c)
        normed[:, columns] = (gated * scale * gain_ref[:, columns]).astype(BF16)

    w_copies[-1].wait_recv()
    for copy in forwards:
        copy.wait_recv()
    for c in range(chunks):
        columns = slice(c * CHUNK, (c + 1) * CHUNK)
        enc_ref[0, :, columns] = dot(normed[...], w_all[:, columns]).astype(BF16)

    encoded = enc_ref[0]
    model = encoded.shape[1]
    queries = latents_ref.shape[0]
    share = queries // n

    def parts_of(values):
        first = values.astype(BF16).astype(F32)
        second = (values - first).astype(BF16).astype(F32)
        third = (values - first - second).astype(BF16).astype(F32)
        return first, second, third

    def tail_of(top, weight):
        at = lax.broadcasted_iota(jnp.int32, (top.shape[0], 128), 1)
        tail = jnp.zeros((top.shape[0], 128), F32)
        for k, part in enumerate(parts_of(top) + parts_of(weight)):
            tail = jnp.where(at == k, part, tail)
        return tail.astype(BF16)

    def read_tail(tail):
        tail = tail.astype(F32)
        top = tail[:, 0:1] + tail[:, 1:2] + tail[:, 2:3]
        return top, tail[:, 3:4] + tail[:, 4:5] + tail[:, 5:6]

    scores = dot(latents_ref[...], encoded, ((1,), (1,))) * (1.0 / math.sqrt(model))
    top = jnp.max(jnp.where(valid, scores, -1e30), axis=1, keepdims=True)
    top = functools.reduce(jnp.add, parts_of(top))
    prob = jnp.where(valid, jnp.exp(scores - top), 0.0)
    weight_sum = jnp.sum(prob, axis=1, keepdims=True)
    tail = tail_of(top, weight_sum).astype(F32).reshape(places, 2, share, 128)
    for s in range(2):
        sum_send[s, :, :, model:] = tail[:, s].astype(BF16)
    prob_low = prob.astype(BF16)
    for c in range(model // CHUNK):
        columns = slice(c * CHUNK, (c + 1) * CHUNK)
        part = dot(prob_low, encoded[:, columns]).reshape(places, 2, share, CHUNK)
        for s in range(2):
            sum_send[s, :, :, columns] = part[:, s].astype(BF16)

    def merge(messages):
        stats = [read_tail(message[:, model:]) for message in messages]
        best = functools.reduce(jnp.maximum, [t for t, _ in stats])
        scales = [jnp.exp(t - best) for t, _ in stats]
        weight = functools.reduce(jnp.add, [w * e for (_, w), e in zip(stats, scales)])
        return best, weight, scales

    def added(messages, scales):
        return functools.reduce(
            jnp.add,
            [message[:, :model].astype(F32) * e for message, e in zip(messages, scales)],
        )

    pair_copies = []
    for step in list(range(1, places)) + [0]:
        target = lax.rem(place + step, places)
        copy = remote(
            sum_send.at[1 - side, target],
            sum_pair.at[step],
            stat_send_sem.at[step],
            stat_recv_sem.at[step],
            seq=partner,
        )
        copy.start()
        pair_copies.append(copy)
    sum_copies = []
    for i, step in enumerate(list(range(1, places)) + [0]):
        target = lax.rem(place + step, places)
        pair_copies[i].wait_recv()
        messages = [sum_send[side, target], sum_pair[step]]
        best, weight, scales = merge(messages)
        sum_both[step, :, :model] = added(messages, scales).astype(BF16)
        sum_both[step, :, model:] = tail_of(best, weight)
        if step > 0:
            copy = remote(
                sum_both.at[step],
                sum_recv.at[step],
                sum_send_sem.at[step],
                sum_recv_sem.at[step],
                seq=2 * target + side,
            )
            copy.start()
            sum_copies.append(copy)
    for copy in sum_copies:
        copy.wait_recv()
    messages = [sum_both[0]] + [sum_recv[step] for step in range(1, places)]
    best, weight, scales = merge(messages)
    inverse = 1.0 / weight
    pool[place, side] = added(messages, [e * inverse for e in scales]).astype(BF16)

    def hand_on(step):
        slot = pool.at[lax.rem(place + places - step, places), side]
        return remote(
            slot, slot, hand_send_sem.at[step], hand_recv_sem.at[step], seq=partner
        )

    pool_copies = []
    for step in range(1, places):
        target = lax.rem(place + step, places)
        copy = remote(
            pool.at[place, side],
            pool.at[place, side],
            pool_send_sem.at[step],
            pool_recv_sem.at[step],
            seq=2 * target + side,
        )
        copy.start()
        pool_copies.append(copy)
    hand_copies = [hand_on(0)]
    hand_copies[0].start()
    for step in range(1, places):
        pool_copies[step - 1].wait_recv()
        copy = hand_on(step)
        copy.start()
        hand_copies.append(copy)
    for copy in hand_copies:
        copy.wait_recv()
    pooled_ref[0] = pool[...].reshape(queries, model)

    for copy in w_copies + forwards + pair_copies + sum_copies + pool_copies + hand_copies:
        copy.wait_send()
    for c in range(chunks):
        pair_copy(c).wait_send()

        @pl.when(along < places - 1)
        def _():
            chain_copy(c).wait_send()

        @pl.when(along > 0)
        def _():
            leaf_copy(c).wait_send()


def body(
    n,
    n_dp,
    ssm_input,
    gate_input,
    state_proj,
    step_raw,
    decay_log,
    skip_gain,
    norm_gain,
    out_weight,
    latents,
    lengths,
):
    rows, width = ssm_input.shape[1], ssm_input.shape[2]
    model = out_weight.shape[1]
    state = state_proj.shape[2] // 4
    queries = latents.shape[0]
    share = queries // n
    chunks = width // CHUNK
    vmem = pl.BlockSpec(memory_space=pltpu.VMEM)
    smem = pl.BlockSpec(memory_space=pltpu.SMEM)
    dma = pltpu.SemaphoreType.DMA
    return pl.pallas_call(
        functools.partial(kernel, n, n_dp),
        out_shape=(
            jax.ShapeDtypeStruct((1, rows, model), BF16),
            jax.ShapeDtypeStruct((1, queries, model), BF16),
        ),
        in_specs=[smem, smem] + [pl.BlockSpec(memory_space=pltpu.HBM)] * 8,
        out_specs=(vmem, vmem),
        scratch_shapes=[
            pltpu.VMEM(ssm_input.shape, BF16),
            pltpu.VMEM(gate_input.shape, BF16),
            pltpu.VMEM(state_proj.shape, BF16),
            pltpu.VMEM(step_raw.shape, F32),
            pltpu.VMEM(decay_log.shape, F32),
            pltpu.VMEM((1, width), F32),
            pltpu.VMEM(latents.shape, BF16),
            pltpu.VMEM((rows, width), F32),
            dma((8,)),
            pltpu.VMEM((width, model), BF16),
            pltpu.VMEM((2, chunks, state, CHUNK), F32),
            pltpu.VMEM((2, chunks, 8, CHUNK), F32),
            pltpu.VMEM((2, chunks, state + 16, CHUNK), BF16),
            pltpu.VMEM((chunks, state + 16, CHUNK), BF16),
            pltpu.VMEM((chunks, state, CHUNK), BF16),
            pltpu.VMEM((chunks, state, CHUNK), BF16),
            pltpu.VMEM((chunks, state, CHUNK), BF16),
            pltpu.VMEM((2, chunks, state, CHUNK), BF16),
            pltpu.VMEM((rows, width), F32),
            pltpu.VMEM((2, rows, width), F32),
            pltpu.VMEM((rows, width), BF16),
            pltpu.VMEM((2, n // 2, share, model + 128), BF16),
            pltpu.VMEM((n // 2, share, model + 128), BF16),
            pltpu.VMEM((n // 2, share, model + 128), BF16),
            pltpu.VMEM((n // 2, share, model + 128), BF16),
            pltpu.VMEM((n // 2, 2, share, model), BF16),
            dma((n_dp,)),
            dma((n_dp,)),
            dma((n_dp,)),
            dma((chunks,)),
            dma((chunks,)),
            dma((chunks,)),
            dma((chunks,)),
            dma((chunks,)),
            dma((chunks,)),
            dma((n // 2,)),
            dma((n // 2,)),
            dma((n // 2,)),
            dma((n // 2,)),
            dma((n // 2,)),
            dma((n // 2,)),
            dma((n // 2,)),
            dma((n // 2,)),
        ],
        compiler_params=pltpu.CompilerParams(
            collective_id=0, has_side_effects=True, vmem_limit_bytes=VMEM_BYTES
        ),
    )(
        lengths,
        skip_gain,
        ssm_input,
        gate_input,
        state_proj,
        step_raw,
        decay_log,
        norm_gain.reshape(1, width),
        out_weight,
        latents,
    )


def solution(mesh):
    in_specs = (
        P("dp", "seq", None),
        P("dp", "seq", None),
        P("dp", "seq", None),
        P("dp", None, "seq"),
        P(),
        P(),
        P(),
        P("dp", None),
        P(),
        P("dp"),
    )
    out_specs = (P("dp", "seq", None), P("dp", None, None))
    return jax.shard_map(
        functools.partial(body, mesh.shape["seq"], mesh.shape["dp"]),
        mesh=mesh,
        in_specs=in_specs,
        out_specs=out_specs,
        check_vma=False,
    )
```
